32 devices in a mesh: ctx: 8 (over z, y), seq: 4 (over x, core).
Axes of the slice: x: 2, y: 2, z: 4, core: 2. Of those that a mesh axis runs over, the one named last changes fastest.
Arguments:
- query_matrix: bfloat16 [32768, 2048], P(('seq', 'ctx')), parts along dimension 0, may hold values from -7 to 7
- key_vectors: bfloat16 [32768, 2048], P(('seq', 'ctx')), parts along dimension 0, may hold values from -7.5 to 7.5
- value_vectors: bfloat16 [32768, 4096], P(('seq', 'ctx')), parts along dimension 0, may hold values from -6 to 6
- input_gate: float32 [8, 32768], P(None, ('seq', 'ctx')), parts along dimension 1, may hold values from -4 to 300
- forget_gate: float32 [8, 32768], P(None, ('seq', 'ctx')), parts along dimension 1, may hold values from 0 to 12.7
Outputs:
- hidden_state: bfloat16 [32768, 4096], P(('seq', 'ctx')), parts along dimension 0
- final_memory: float32 [32, 256, 512], P('seq', 'ctx'), parts along dimension 0
- final_normalizer: float32 [32, 256], P('seq', 'ctx'), parts along dimension 0
- final_stabilizer: float32 [32], P('seq'), parts along dimension 0
The draws below stay inside these ranges and needn't reach their ends.
There are 4 independent parts, one for each index of `seq`. The reference program is written for one: setup_inputs(seed, part) draws one part's arguments, and reference() takes and returns one part's arrays. A program takes and returns all parts, laid end to end along the dimension named above; each array names one. Nothing has to cross between parts.
All inputs are finite; a program needn't handle non-finite values.
Results may differ from the reference program's by a relative error of at most 0.0056.
Values sent between devices are 32-bit elements; how exact they have to be, the bound alone decides.
No kernel may reach another device: no remote copies, remote signals or barrier semaphores. Data moves between devices by JAX's collectives and lax.ppermute only.
A program may use at most 192 MiB of HBM per device.

```python
import math
import jax
import jax.numpy as jnp
from jax import lax

H = 8
DQK = 256
DV = 512
TOK_DEV = 1024
TOKENS = 8192
N_CTX = 8


def draw_query_matrix(key, part):
    base = jnp.clip(jax.random.normal(jax.random.fold_in(key, 21), (TOKENS, H * DQK), jnp.float32), -6.0, 6.0)
    return base.astype(jnp.bfloat16)


def draw_key_vectors(key, part):
    base = jnp.clip(jax.random.normal(jax.random.fold_in(key, 22), (TOKENS, H * DQK), jnp.float32), -6.0, 6.0)
    return base.astype(jnp.bfloat16)


def draw_forget_gate(key, part):
    subkeys = jax.random.split(key, 6)
    order = jax.random.permutation(subkeys[0], H)
    slow = order < H // 2
    base = jnp.where(slow, jax.random.uniform(subkeys[1], (H,), jnp.float32, 10.0, 12.0), jax.random.uniform(subkeys[2], (H,), jnp.float32, 2.5, 4.5))
    coarse_estimate = base[:, None] + jax.random.uniform(subkeys[3], (H, TOKENS), jnp.float32, -0.7, 0.7)
    spots = jax.random.randint(subkeys[4], (3,), 0, TOKENS)
    gate_magnitudes = jax.random.uniform(subkeys[5], (3,), jnp.float32, 0.0, 1.4)
    places = jnp.arange(TOKENS)
    spike_positions = places[None, :] == spots[:, None]
    sudden_surge = jnp.max(jnp.where(spike_positions, gate_magnitudes[:, None], -1.0), axis=0)
    return jnp.where(sudden_surge[None, :] >= 0.0, sudden_surge[None, :], coarse_estimate).astype(jnp.float32)


def draw_input_gate(key, part):
    subkeys = jax.random.split(key, 1)
    base = jax.random.uniform(subkeys[0], (H, TOKENS), jnp.float32, -4.0, 2.0)
    return base.astype(jnp.float32)


def steps_of(stream_key, shape, shards, least, high):
    def one(dim, parts):
        steps = jax.random.uniform(jax.random.fold_in(jax.random.fold_in(stream_key, 6), dim), (parts,), jnp.float32, least / len(shards), high / len(shards))
        return jnp.repeat(jnp.exp(steps), shape[dim] // parts).reshape((-1,) + (1,) * (len(shape) - dim - 1))

    loudness = one(*shards[0])
    for cut in shards[1:]:
        loudness = loudness * one(*cut)
    return loudness


def noise(rng, dims, spread, most, pieces=(), held_as=jnp.bfloat16):
    values = spread * jax.random.normal(rng, dims, jnp.float32)
    if pieces:
        values = values * steps_of(rng, dims, pieces, -0.22, 0.18)
    return jnp.clip(values, -most, most).astype(held_as)


def setup_inputs(seed: int = 0, part: int = 0) -> dict:
    splits = jax.random.split(jax.random.key(seed), 6)
    part_keys = jax.random.split(jax.random.fold_in(splits[5], part), 6)
    return {
        "query_matrix": draw_query_matrix(jax.random.fold_in(jax.random.fold_in(splits[5], part), 71), part),
        "key_vectors": draw_key_vectors(jax.random.fold_in(jax.random.fold_in(splits[5], part), 71), part),
        "value_vectors": noise(part_keys[2], (TOKENS, H * DV), 1.0, 6.0, ((0, 8),)),
        "input_gate": draw_input_gate(jax.random.fold_in(jax.random.fold_in(splits[5], part), 71), part),
        "forget_gate": draw_forget_gate(jax.random.fold_in(jax.random.fold_in(splits[5], part), 71), part),
    }


VERY_NEGATIVE = -1e+30

def summarize(key_vectors, value_vectors, input_gate, cumulated):
    decay_sum = cumulated[:, -1]
    exponent = decay_sum[:, None] - cumulated + input_gate
    stabilizer = lax.optimization_barrier(jnp.max(exponent, axis=1))
    weight = jnp.exp(exponent - stabilizer[:, None])

    def one_head(head_index):
        key_rows = lax.dynamic_slice_in_dim(key_vectors, head_index * DQK, DQK, 1).astype(jnp.float32)
        value_rows = lax.dynamic_slice_in_dim(value_vectors, head_index * DV, DV, 1)
        scaled = key_rows * weight[head_index][:, None]
        matrix_memory = lax.dot_general(scaled.astype(jnp.bfloat16), value_rows, (((0,), (0,)), ((), ())), preferred_element_type=jnp.float32)
        return (matrix_memory, lax.optimization_barrier(jnp.sum(scaled, axis=0)))
    matrix_memory, normal = lax.map(one_head, jnp.arange(H, dtype=jnp.int32))
    return (matrix_memory, normal, stabilizer, decay_sum)

def combine(earlier, later):
    first_memory, first_normal, first_stab, first_decay = earlier
    second_memory, second_normal, second_stab, second_decay = later
    stabilizer = jnp.maximum(first_stab + second_decay, second_stab)
    first_scale = jnp.exp(first_stab + second_decay - stabilizer)
    second_scale = jnp.exp(second_stab - stabilizer)
    matrix_memory = first_memory * first_scale[..., None, None] + second_memory * second_scale[..., None, None]
    normal = first_normal * first_scale[..., None] + second_normal * second_scale[..., None]
    return (matrix_memory, normal, stabilizer, first_decay + second_decay)

def block_output(query_matrix, key_vectors, value_vectors, input_gate, cumulated, prefix_memory, prefix_normal, prefix_stab):
    length = query_matrix.shape[0]
    scaling = 1.0 / math.sqrt(DQK)
    memory_b = prefix_memory.astype(jnp.bfloat16)
    row_index = lax.broadcasted_iota(jnp.int32, (length, length), 0)
    col_index = lax.broadcasted_iota(jnp.int32, (length, length), 1)
    causal = row_index >= col_index

    def one_head(head_index, out_buffer):
        head_index = jnp.asarray(head_index).astype(jnp.int32)
        query_rows = lax.dynamic_slice_in_dim(query_matrix, head_index * DQK, DQK, 1)
        key_rows = lax.dynamic_slice_in_dim(key_vectors, head_index * DQK, DQK, 1)
        value_rows = lax.dynamic_slice_in_dim(value_vectors, head_index * DV, DV, 1)
        scores = lax.dot_general(query_rows, key_rows, (((1,), (1,)), ((), ())), preferred_element_type=jnp.float32) * scaling
        cum_head = cumulated[head_index]
        gate_head = input_gate[head_index]
        exponent = jnp.where(causal, cum_head[:, None] - cum_head[None, :] + gate_head[None, :], VERY_NEGATIVE)
        carried = cum_head + prefix_stab[head_index]
        stabilizer = jnp.maximum(carried, lax.optimization_barrier(jnp.max(exponent, axis=1)))
        weights = jnp.where(causal, jnp.exp(exponent - stabilizer[:, None]) * scores, 0.0)
        factor = jnp.exp(carried - stabilizer)
        carried_term = jnp.dot(query_rows, memory_b[head_index], preferred_element_type=jnp.float32) * scaling
        numerator = factor[:, None] * carried_term + jnp.dot(weights.astype(jnp.bfloat16), value_rows, preferred_element_type=jnp.float32)
        query_normal = lax.optimization_barrier(jnp.sum(query_rows.astype(jnp.float32) * prefix_normal[head_index][None, :], axis=1)) * scaling
        denominator = factor * query_normal + lax.optimization_barrier(jnp.sum(weights, axis=1))
        result = numerator / jnp.maximum(jnp.abs(denominator), jnp.exp(-stabilizer))[:, None]
        return lax.dynamic_update_slice_in_dim(out_buffer, result.astype(jnp.bfloat16), head_index * DV, 1)
    return lax.fori_loop(0, H, one_head, jnp.zeros((length, H * DV), jnp.bfloat16))

def reference(query_matrix, key_vectors, value_vectors, input_gate, forget_gate):
    log_forget = jax.nn.log_sigmoid(forget_gate)
    cumulated = jnp.cumsum(log_forget.reshape(H, N_CTX, TOK_DEV).transpose(1, 0, 2), axis=2)
    gate_blocks = input_gate.reshape(H, N_CTX, TOK_DEV).transpose(1, 0, 2)
    query_segments = query_matrix.reshape(N_CTX, TOK_DEV, H * DQK)
    key_blocks = key_vectors.reshape(N_CTX, TOK_DEV, H * DQK)
    value_blocks = value_vectors.reshape(N_CTX, TOK_DEV, H * DV)
    identity = (jnp.zeros((H, DQK, DV), jnp.float32), jnp.zeros((H, DQK), jnp.float32), jnp.full((H,), VERY_NEGATIVE, jnp.float32), jnp.zeros((H,), jnp.float32))

    def advance(prefix, block_data):
        queries_here, keys_here, values_here, gates_here, cum_here = block_data
        output = block_output(queries_here, keys_here, values_here, gates_here, cum_here, prefix[0], prefix[1], prefix[2])
        own_summary = summarize(keys_here, values_here, gates_here, cum_here)
        return (combine(prefix, own_summary), output)
    final_state, outputs = lax.scan(advance, identity, (query_segments, key_blocks, value_blocks, gate_blocks, cumulated))
    return (outputs.reshape(TOKENS, H * DV), final_state[0], final_state[1], final_state[2])
```

```python
import functools

import jax
import jax.numpy as jnp
from jax import lax
from jax.experimental import pallas as pl
from jax.experimental.pallas import tpu as pltpu
from jax.sharding import PartitionSpec as P

VERY_NEGATIVE = -1e30
LANES = 128
MIB = 1 << 20

ROW_A, ROW_B, ROW_KEEP, ROW_RECV, ROW_SEND_P, ROW_SEND_S, ROW_OWN_P, ROW_OWN_S, ROW_FIN_P, ROW_FIN_L = range(10)
TABLE_ROWS = 16


def params(mib):
    return pltpu.CompilerParams(vmem_limit_bytes=mib * MIB)


def cost(flops, bytes_accessed, transcendentals=0):
    return pl.CostEstimate(
        flops=int(flops), bytes_accessed=int(bytes_accessed), transcendentals=int(transcendentals)
    )


def lane_iota(shape):
    return lax.broadcasted_iota(jnp.int32, shape, len(shape) - 1)


def pick_lane(block, lane):
    return jnp.sum(jnp.where(lane_iota(block.shape) == lane, block, 0.0), axis=1, keepdims=True)


def gates_kernel(input_ref, forget_ref, rows_ref, columns_ref, stats_ref):
    heads, tokens = input_ref.shape
    gate = forget_ref[...]
    cumulated = jnp.minimum(gate, 0.0) - jnp.log1p(jnp.exp(-jnp.abs(gate)))
    lanes = lane_iota((heads, tokens))
    step = 1
    while step < tokens:
        cumulated = cumulated + jnp.where(lanes >= step, pltpu.roll(cumulated, step, 1), 0.0)
        step *= 2
    level = input_ref[...] - cumulated
    running = level
    step = 1
    while step < tokens:
        running = jnp.maximum(
            running, jnp.where(lanes >= step, pltpu.roll(running, step, 1), VERY_NEGATIVE)
        )
        step *= 2
    highest = jnp.max(level, axis=1, keepdims=True)
    decay = cumulated[:, tokens - 1 : tokens]
    weight = jnp.exp(level - highest)
    rows_ref[...] = level
    filler = jnp.zeros((LANES - 3 * heads, tokens), jnp.float32)
    columns_ref[...] = jnp.concatenate([weight, running, cumulated, filler], axis=0).T
    lane = lane_iota((heads, LANES))
    stats_ref[...] = jnp.where(lane == 0, decay + highest, jnp.where(lane == 1, decay, 0.0))


def gates(input_gate, forget_gate):
    heads, tokens = input_gate.shape
    return pl.pallas_call(
        gates_kernel,
        out_shape=(
            jax.ShapeDtypeStruct((heads, tokens), jnp.float32),
            jax.ShapeDtypeStruct((tokens, LANES), jnp.float32),
            jax.ShapeDtypeStruct((heads, LANES), jnp.float32),
        ),
        cost_estimate=cost(1e6, 1e6),
        name="gates",
    )(input_gate, forget_gate)


def summary_of(head, key_ref, value_ref, columns_ref):
    weight = pick_lane(columns_ref[...], head)
    scaled = key_ref[...].astype(jnp.float32) * weight
    memory = lax.dot_general(
        scaled.astype(jnp.bfloat16),
        value_ref[...],
        (((0,), (0,)), ((), ())),
        preferred_element_type=jnp.float32,
    )
    return memory, jnp.sum(scaled, axis=0, keepdims=True)


def summary_kernel(first_ref, key_ref, value_ref, columns_ref, normal_ref, *memory_refs, count):
    turn = pl.program_id(0)
    memory, normal = summary_of(first_ref[0] + turn, key_ref, value_ref, columns_ref)
    normal_ref[0] = normal
    half = memory.shape[1] // 2
    for place in range(count):

        @pl.when(turn == place)
        def _():
            memory_refs[2 * place][...] = memory[:, :half]
            memory_refs[2 * place + 1][...] = memory[:, half:]


def summaries(first, count, keys, values, columns, dqk, dv):
    tokens = keys.shape[0]
    half = dv // 2
    outs = pl.pallas_call(
        functools.partial(summary_kernel, count=count),
        grid_spec=pltpu.PrefetchScalarGridSpec(
            num_scalar_prefetch=1,
            grid=(count,),
            in_specs=[
                pl.BlockSpec((tokens, dqk), lambda i, f: (0, f[0] + i)),
                pl.BlockSpec((tokens, dv), lambda i, f: (0, f[0] + i)),
                pl.BlockSpec((tokens, LANES), lambda i, f: (0, 0)),
            ],
            out_specs=[pl.BlockSpec((1, 1, dqk), lambda i, f: (i, 0, 0))]
            + [pl.BlockSpec((dqk, half), lambda i, f: (0, 0))] * (2 * count),
        ),
        out_shape=[jax.ShapeDtypeStruct((count, 1, dqk), jnp.float32)]
        + [jax.ShapeDtypeStruct((dqk, half), jnp.float32)] * (2 * count),
        compiler_params=params(32),
        cost_estimate=cost(
            2 * count * tokens * dqk * dv, count * (2 * tokens * (dqk + dv) + 4 * dqk * dv)
        ),
        name="summaries",
    )(first, keys, values, columns)
    return outs[0], outs[1:]


def weights_kernel(place_ref, gathered_ref, table_ref, prefix_ref, final_ref, tops_ref, *, blocks, skew):
    heads = gathered_ref.shape[1]
    dqk = gathered_ref.shape[2] - LANES
    lane_heads = heads // 2
    levels = blocks // 2
    place = place_ref[0]
    side = lax.rem(place, 2)
    level = lax.div(place, 2)

    tops, decays, normals = [], [], []
    for block in range(blocks):
        held = gathered_ref[lax.rem(block - place + blocks, blocks)]
        normals.append(held[:, :dqk])
        tops.append(held[:, dqk : dqk + 1])
        decays.append(held[:, dqk + 1 : dqk + 2])

    pick = lambda at, value, otherwise: jnp.where(level == at, value, otherwise)
    top = jnp.full((heads, 1), VERY_NEGATIVE, jnp.float32)
    normal = jnp.zeros((heads, dqk), jnp.float32)
    zero = jnp.zeros((heads, 1), jnp.float32)
    mine_a = mine_b = mine_first = mine_second = zero
    carry_p = carry_s = zero
    prefix_top, prefix_normal = zero, normal
    own_top = top
    scales = []
    for z in range(levels):
        t0, t1, d0, d1 = tops[2 * z], tops[2 * z + 1], decays[2 * z], decays[2 * z + 1]
        pair_top = jnp.maximum(t0 + d1, t1)
        first, second = jnp.exp(t0 + d1 - pair_top), jnp.exp(t1 - pair_top)
        pair_normal = normals[2 * z] * first + normals[2 * z + 1] * second
        middle_top = jnp.maximum(top + d0, t0)
        alpha, beta = jnp.exp(top + d0 - middle_top), jnp.exp(t0 - middle_top)
        middle_normal = normal * alpha + normals[2 * z] * beta
        pair_decay = d0 + d1
        next_top = jnp.maximum(top + pair_decay, pair_top)
        a, b = jnp.exp(top + pair_decay - next_top), jnp.exp(pair_top - next_top)
        mine_a, mine_b = pick(z, a, mine_a), pick(z, b, mine_b)
        mine_first, mine_second = pick(z, first, mine_first), pick(z, second, mine_second)
        carry_p, carry_s = pick(z, alpha, carry_p), pick(z, beta, carry_s)
        prefix_top = pick(z, jnp.where(side == 0, top, middle_top), prefix_top)
        prefix_normal = pick(z, jnp.where(side == 0, normal, middle_normal), prefix_normal)
        normal = normal * a + pair_normal * b
        top = next_top
        scales.append((a, b))
    later = jnp.ones((heads, 1), jnp.float32)
    final_p = final_l = zero
    for z in reversed(range(levels)):
        a, b = scales[z]
        final_l = pick(z, b * later, final_l)
        later = later * a
        final_p = pick(z, later, final_p)

    one = jnp.ones((heads, 1), jnp.float32)
    by_side = lambda zero_value, one_value: jnp.where(side == 0, zero_value, one_value)
    lanes = lane_iota((heads, LANES))
    rows = lax.broadcasted_iota(jnp.int32, (heads, LANES), 0)
    head_of_chunk = lane_heads * side + lax.div(lanes, 2)
    head_of_step = lane_heads * side + lax.div(
        jnp.clip(lanes - skew * level, 0, 2 * lane_heads - 1), 2
    )

    def spread(column, heads_wanted):
        return jnp.sum(jnp.where(rows == heads_wanted, column, 0.0), axis=0, keepdims=True)

    entries = {
        ROW_A: spread(mine_a, head_of_step),
        ROW_B: spread(mine_b, head_of_step),
        ROW_KEEP: spread(by_side(mine_first, mine_second), head_of_chunk),
        ROW_RECV: spread(by_side(mine_second, mine_first), head_of_chunk),
        ROW_SEND_P: spread(by_side(carry_p, one), head_of_chunk),
        ROW_SEND_S: spread(by_side(carry_s, zero), head_of_chunk),
        ROW_OWN_P: spread(by_side(one, carry_p), head_of_chunk),
        ROW_OWN_S: spread(by_side(zero, carry_s), head_of_chunk),
        ROW_FIN_P: spread(final_p, head_of_chunk),
        ROW_FIN_L: spread(final_l, head_of_chunk),
    }
    empty = jnp.zeros((1, LANES), jnp.float32)
    table_ref[...] = jnp.concatenate([entries.get(r, empty) for r in range(TABLE_ROWS)], axis=0)
    prefix_ref[...] = prefix_normal
    final_ref[...] = normal
    tops_ref[...] = jnp.where(lanes == 0, prefix_top, jnp.where(lanes == 1, top, 0.0))


def weights(place, gathered, skew):
    blocks, heads, width = gathered.shape
    dqk = width - LANES
    return pl.pallas_call(
        functools.partial(weights_kernel, blocks=blocks, skew=skew),
        grid_spec=pltpu.PrefetchScalarGridSpec(
            num_scalar_prefetch=1,
            grid=(1,),
            in_specs=[pl.BlockSpec((blocks, heads, width), lambda i, p: (0, 0, 0))],
            out_specs=[
                pl.BlockSpec((TABLE_ROWS, LANES), lambda i, p: (0, 0)),
                pl.BlockSpec((heads, dqk), lambda i, p: (0, 0)),
                pl.BlockSpec((heads, dqk), lambda i, p: (0, 0)),
                pl.BlockSpec((heads, LANES), lambda i, p: (0, 0)),
            ],
        ),
        out_shape=[
            jax.ShapeDtypeStruct((TABLE_ROWS, LANES), jnp.float32),
            jax.ShapeDtypeStruct((heads, dqk), jnp.float32),
            jax.ShapeDtypeStruct((heads, dqk), jnp.float32),
            jax.ShapeDtypeStruct((heads, LANES), jnp.float32),
        ],
        cost_estimate=cost(1e6, 1e6),
        name="weights",
    )(place, gathered)


def attention_kernel(query_ref, key_ref, value_ref, rows_ref, columns_ref, *rest, first):
    out_ref, sums_ref = rest[-2:]
    turn = pl.program_id(0)
    head = first + turn
    tokens = query_ref.shape[0]
    heads = rows_ref.shape[0]
    tile = min(256, tokens)
    level = rows_ref[pl.ds(head, 1), :]
    lanes = lane_iota((tile, LANES))
    rows = lax.broadcasted_iota(jnp.int32, (tile, tile), 0)
    causal = rows >= lax.broadcasted_iota(jnp.int32, (tile, tile), 1)

    @pl.when(turn == 0)
    def _():
        sums_ref[...] = jnp.zeros_like(sums_ref)

    for start in range(0, tokens, tile):
        stop = start + tile
        here = pl.ds(start, tile)
        query = query_ref[here, :]
        running = pick_lane(columns_ref[here, :], heads + head)
        scores = lax.dot_general(
            query, key_ref[:stop, :], (((1,), (1,)), ((), ())), preferred_element_type=jnp.float32
        )
        attn = jnp.exp(level[:, :stop] - running) * scores
        last = jnp.where(causal, attn[:, start:], 0.0)
        attn = jnp.concatenate([attn[:, :start], last], axis=1) if start else last
        total = jnp.sum(attn, axis=1, keepdims=True)
        sums_ref[here, :] = jnp.where(lanes == head, total, sums_ref[here, :])
        out_ref[here, :] = jnp.dot(
            attn.astype(jnp.bfloat16), value_ref[:stop, :], preferred_element_type=jnp.float32
        ).astype(jnp.bfloat16)


def attention(first, count, queries, keys, values, rows, columns, held, dqk, dv):
    tokens = queries.shape[0]
    heads = rows.shape[0]
    in_specs = [
        pl.BlockSpec((tokens, dqk), lambda i: (0, first + i)),
        pl.BlockSpec((tokens, dqk), lambda i: (0, first + i)),
        pl.BlockSpec((tokens, dv), lambda i: (0, first + i)),
        pl.BlockSpec((heads, tokens), lambda i: (0, 0)),
        pl.BlockSpec((tokens, LANES), lambda i: (0, 0)),
    ]
    operands = [queries, keys, values, rows, columns]
    aliases = {}
    if held is not None:
        in_specs.append(pl.BlockSpec(memory_space=pl.ANY))
        operands.append(held)
        aliases = {5: 0}
    return pl.pallas_call(
        functools.partial(attention_kernel, first=first),
        grid=(count,),
        in_specs=in_specs,
        out_specs=[
            pl.BlockSpec((tokens, dv), lambda i: (0, first + i)),
            pl.BlockSpec((tokens, LANES), lambda i: (0, 0)),
        ],
        out_shape=[
            jax.ShapeDtypeStruct((tokens, heads * dv), jnp.bfloat16),
            jax.ShapeDtypeStruct((tokens, LANES), jnp.float32),
        ],
        input_output_aliases=aliases,
        compiler_params=params(32),
        cost_estimate=cost(
            2 * count * tokens * tokens * (dqk + dv) * 0.8, count * 4 * tokens * (dqk + dv)
        ),
        name="attention",
    )(*operands)


def factors_kernel(query_ref, columns_ref, normal_ref, tops_ref, *rest):
    *sums_refs, out_ref, product_ref = rest
    head = pl.program_id(0)
    heads, dqk = normal_ref.shape
    tokens = query_ref.shape[0]

    normal = normal_ref[...]
    high = normal.astype(jnp.bfloat16).astype(jnp.float32)
    middle = (normal - high).astype(jnp.bfloat16).astype(jnp.float32)
    low = normal - high - middle
    filler = jnp.zeros((LANES - 3 * heads, dqk), jnp.float32)
    parts = jnp.concatenate([high, middle, low, filler], axis=0).T
    lanes = lane_iota((dqk, LANES))
    parts = jnp.where((lanes < 3 * heads) & (lax.rem(lanes, heads) == head), parts, 0.0)
    product = jnp.dot(
        query_ref[...], parts.astype(jnp.bfloat16), preferred_element_type=jnp.float32
    )

    @pl.when(head == 0)
    def _():
        product_ref[...] = product

    @pl.when(head > 0)
    def _():
        product_ref[...] += product

    @pl.when(head == heads - 1)
    def _():
        lane = lane_iota((tokens, LANES))
        shift = lambda block, by: pltpu.roll(block, (LANES - by) % LANES, 1)
        product = product_ref[...]
        product = product + shift(product, heads) + shift(product, 2 * heads)
        top = jnp.concatenate(
            [tops_ref[...], jnp.zeros((LANES - heads, LANES), jnp.float32)], axis=0
        ).T[0:1, :]
        running, cumulated = shift(columns_ref[...], heads), shift(columns_ref[...], 2 * heads)
        total = sums_refs[0][...]
        for ref in sums_refs[1:]:
            total = total + ref[...]
        highest = jnp.maximum(running, top)
        scaling = float(dqk) ** -0.5
        local, carried = jnp.exp(running - highest), jnp.exp(top - highest)
        denominator = (local * total + carried * product) * scaling
        divisor = jnp.maximum(jnp.abs(denominator), jnp.exp(-(cumulated + highest)))
        local, carried = local * scaling / divisor, carried * scaling / divisor
        out_ref[...] = jnp.where(lane < heads, local, pltpu.roll(carried, heads, 1))


def factors(queries, columns, normal, tops, sums):
    tokens = queries.shape[0]
    heads, dqk = normal.shape
    whole = lambda shape: pl.BlockSpec(shape, lambda i: (0,) * len(shape))
    return pl.pallas_call(
        factors_kernel,
        grid=(heads,),
        in_specs=[
            pl.BlockSpec((tokens, dqk), lambda i: (0, i)),
            whole((tokens, LANES)),
            whole((heads, dqk)),
            whole((heads, LANES)),
        ]
        + [whole((tokens, LANES))] * len(sums),
        out_specs=whole((tokens, LANES)),
        out_shape=jax.ShapeDtypeStruct((tokens, LANES), jnp.float32),
        scratch_shapes=[pltpu.VMEM((tokens, LANES), jnp.float32)],
        compiler_params=params(24),
        cost_estimate=cost(2 * tokens * heads * dqk * 512, 2 * tokens * heads * dqk),
        name="factors",
    )(queries, columns, normal, tops, *sums)


def finish_kernel(block_ref, query_ref, factors_ref, held_ref, *rest, dv_blocks, heads):
    *memory_refs, out_ref = rest
    turn = pl.program_id(0)
    head = lax.div(block_ref[0] + turn, dv_blocks)
    local = pick_lane(factors_ref[...], head)
    carried = pick_lane(factors_ref[...], heads + head)
    for place, memory_ref in enumerate(memory_refs):

        @pl.when(turn == place)
        def _():
            term = jnp.dot(
                query_ref[...],
                memory_ref[...].astype(jnp.bfloat16),
                preferred_element_type=jnp.float32,
            )
            out_ref[...] = (held_ref[...].astype(jnp.float32) * local + term * carried).astype(
                out_ref.dtype
            )


def finish(first_block, memories, queries, factor, held, heads):
    tokens = queries.shape[0]
    dqk, half = memories[0].shape
    count = len(memories)
    return pl.pallas_call(
        functools.partial(finish_kernel, dv_blocks=2, heads=heads),
        grid_spec=pltpu.PrefetchScalarGridSpec(
            num_scalar_prefetch=1,
            grid=(count,),
            in_specs=[
                pl.BlockSpec((tokens, dqk), lambda i, b: (0, lax.div(b[0] + i, 2))),
                pl.BlockSpec((tokens, LANES), lambda i, b: (0, 0)),
                pl.BlockSpec((tokens, half), lambda i, b: (0, b[0] + i)),
            ]
            + [pl.BlockSpec((dqk, half), lambda i, b: (0, 0))] * count,
            out_specs=pl.BlockSpec((tokens, half), lambda i, b: (0, b[0] + i)),
        ),
        out_shape=jax.ShapeDtypeStruct(held.shape, held.dtype),
        input_output_aliases={3: 0},
        compiler_params=params(24),
        cost_estimate=cost(
            2 * count * tokens * dqk * half, count * (2 * tokens * (dqk + 2 * half) + 4 * dqk * half)
        ),
        name="finish",
    )(first_block, queries, factor, held, *memories)


def down_kernel(level_ref, table_ref, *refs, chunks, first):
    level_refs = refs[:chunks]
    out_ref = refs[-1]
    for c in range(chunks):
        value = level_refs[c][...] * table_ref[ROW_FIN_L, c]
        out_ref[c] = value if first else value + refs[chunks][c]


def down(target, table, level_memories, earlier, rows):
    chunks = len(level_memories)
    half = level_memories[0].shape[1]
    operands = list(level_memories)
    in_specs = [pl.BlockSpec(memory_space=pltpu.SMEM)]
    in_specs += [pl.BlockSpec((rows, half), lambda i, t: (t[0], 0))] * chunks
    if earlier is not None:
        operands.append(earlier)
        in_specs.append(pl.BlockSpec((chunks, rows, half), lambda i, t: (0, 0, 0)))
    return pl.pallas_call(
        functools.partial(down_kernel, chunks=chunks, first=earlier is None),
        grid_spec=pltpu.PrefetchScalarGridSpec(
            num_scalar_prefetch=1,
            grid=(1,),
            in_specs=in_specs,
            out_specs=pl.BlockSpec((chunks, rows, half), lambda i, t: (0, 0, 0)),
        ),
        out_shape=jax.ShapeDtypeStruct((chunks, rows, half), jnp.float32),
        cost_estimate=cost(1e6, 12 * chunks * rows * half),
        name="down",
    )(target, table, *operands)


def final_kernel(level_ref, side_ref, table_ref, *refs, chunks):
    level_refs, own_refs, send_refs = refs[:chunks], refs[chunks : 2 * chunks], refs[2 * chunks : 3 * chunks]
    above_ref, keep_out, send_out = refs[3 * chunks :]
    side = side_ref[0]
    rows = keep_out.shape[1]
    half = level_refs[0].shape[1]
    for c in range(chunks):
        prefix = jnp.where(side == 0, own_refs[c][...], send_refs[c][...])
        value = (
            prefix * table_ref[ROW_FIN_P, c]
            + level_refs[c][...] * table_ref[ROW_FIN_L, c]
            + above_ref[c]
        )
        low, high = value[:rows], value[rows:]
        columns = pl.ds((c % 2) * half, half)
        keep_out[c // 2, :, columns] = jnp.where(side == 0, low, high)
        send_out[c // 2, :, columns] = jnp.where(side == 0, high, low)


def final_rows(level, side, table, level_memories, owns, sends, above):
    chunks = len(level_memories)
    dqk, half = level_memories[0].shape
    rows = above.shape[1]
    out = jax.ShapeDtypeStruct((chunks // 2, rows // 2, 2 * half), jnp.float32)
    return pl.pallas_call(
        functools.partial(final_kernel, chunks=chunks),
        grid_spec=pltpu.PrefetchScalarGridSpec(
            num_scalar_prefetch=2,
            grid=(1,),
            in_specs=[pl.BlockSpec(memory_space=pltpu.SMEM)]
            + [pl.BlockSpec((rows, half), lambda i, t, s: (t[0], 0))] * (3 * chunks)
            + [pl.BlockSpec((chunks, rows, half), lambda i, t, s: (0, 0, 0))],
            out_specs=[pl.BlockSpec(out.shape, lambda i, t, s: (0, 0, 0))] * 2,
        ),
        out_shape=[out, out],
        cost_estimate=cost(1e6, 20 * chunks * rows * half),
        name="final_rows",
    )(level, side, table, *level_memories, *owns, *sends, above)


SKEW = 2


def shards(queries, keys, values, input_gate, forget_gate, *, blocks):
    heads = input_gate.shape[0]
    dqk, dv = queries.shape[1] // heads, values.shape[1] // heads
    lane_heads = heads // 2
    levels = blocks // 2
    chunks = 2 * lane_heads
    place = lax.axis_index("ctx")
    side, level = lax.rem(place, 2), lax.div(place, 2)
    across = [(i, i ^ 1) for i in range(blocks)]
    up = [(i, i + 2) for i in range(blocks - 2)]
    downward = [(i + 2, i) for i in range(blocks - 2)]
    send = lambda value, pairs: lax.ppermute(value, "ctx", pairs)
    scalar = lambda value: jnp.reshape(value, (1,)).astype(jnp.int32)

    own_first, other_first = lane_heads * side, lane_heads * (1 - side)
    rows, columns, stats = gates(input_gate, forget_gate)
    normal_0, away = summaries(scalar(other_first), 1, keys, values, columns, dqk, dv)
    received = [send(a, across) for a in away]
    if lane_heads > 1:
        normal_1, away = summaries(
            scalar(other_first + 1), lane_heads - 1, keys, values, columns, dqk, dv
        )
        received += [send(a, across) for a in away]
        normal_0 = jnp.concatenate([normal_0, normal_1], axis=0)
    normal_own, kept = summaries(scalar(own_first), lane_heads, keys, values, columns, dqk, dv)

    ordered = jnp.where(
        side == 0,
        jnp.concatenate([normal_own, normal_0], axis=0),
        jnp.concatenate([normal_0, normal_own], axis=0),
    ).reshape(heads, dqk)
    gathered = jnp.concatenate([ordered, stats], axis=1)[None]
    while gathered.shape[0] < blocks:
        reach = gathered.shape[0]
        more = send(gathered, [(i, (i - reach) % blocks) for i in range(blocks)])
        gathered = jnp.concatenate([gathered, more], axis=0)[:blocks]
    table, prefix_normal, final_normal, tops = weights(scalar(place), gathered, SKEW)
    entry = lambda row, lane: lax.slice(table, (row, lane), (row + 1, lane + 1))

    held, sums = None, []
    group = 2 if heads % 2 == 0 else 1
    for first in range(0, heads, group):
        held, total = attention(first, group, queries, keys, values, rows, columns, held, dqk, dv)
        sums.append(total)
    factor = factors(queries, columns, prefix_normal, tops, sums)

    pair = [
        kept[c] * entry(ROW_KEEP, c) + received[c] * entry(ROW_RECV, c) for c in range(chunks)
    ]

    def by_level(options):
        result = None
        for z, value in enumerate(options):
            if value is None:
                continue
            result = value if result is None else jnp.where(level == z, value, result)
        return result

    at = lambda items, index: items[index] if 0 <= index < len(items) else None
    steps = chunks + SKEW * (levels - 2)
    arrived = []
    for s in range(steps):
        mine = by_level([at(pair, s - SKEW * z) for z in range(levels - 1)])
        value = mine * entry(ROW_B, s)
        if s >= SKEW:
            value = value + arrived[s - SKEW] * entry(ROW_A, s)
        arrived.append(send(value, up))

    sends, owns, others = [], [], []
    for c in range(chunks):
        prefix = by_level([None] + [arrived[c + SKEW * (z - 1)] for z in range(1, levels)])
        prefix = jnp.where(level == 0, 0.0, prefix)
        sends.append(prefix * entry(ROW_SEND_P, c) + kept[c] * entry(ROW_SEND_S, c))
        owns.append(prefix * entry(ROW_OWN_P, c) + received[c] * entry(ROW_OWN_S, c))
        others.append(send(sends[c], across))

    above = None
    rows_of_level = dqk // levels
    for d in range(1, levels):
        target = jnp.maximum(d - levels + level, 0)
        above = send(down(scalar(target), table, pair, above, rows_of_level), downward)
    keep_rows, send_rows = final_rows(scalar(level), scalar(side), table, pair, owns, sends, above)
    other_rows = send(send_rows, across)
    final_memory = jnp.where(
        side == 0,
        jnp.concatenate([keep_rows, other_rows], axis=0),
        jnp.concatenate([other_rows, keep_rows], axis=0),
    )
    share = dqk // blocks
    final_normalizer = lax.dynamic_slice_in_dim(final_normal, place * share, share, 1)
    final_stabilizer = tops[:, 1]

    hidden = held
    for c in range(0, chunks, 2):
        hidden = finish(scalar(2 * own_first + c), owns[c : c + 2], queries, factor, hidden, heads)
    for c in range(chunks):
        hidden = finish(scalar(2 * other_first + c), others[c : c + 1], queries, factor, hidden, heads)
    return hidden, final_memory, final_normalizer, final_stabilizer


def solution(mesh):
    token_spec = P(("seq", "ctx"), None)
    gate_spec = P(None, ("seq", "ctx"))
    return jax.shard_map(
        functools.partial(shards, blocks=mesh.shape["ctx"]),
        mesh=mesh,
        in_specs=(token_spec, token_spec, token_spec, gate_spec, gate_spec),
        out_specs=(token_spec, P("seq", "ctx", None), P("seq", "ctx"), P("seq")),
        check_vma=False,
    )
```

```python
import functools

import jax
import jax.numpy as jnp
from jax import lax
from jax.experimental import pallas as pl
from jax.experimental.pallas import tpu as pltpu
from jax.sharding import PartitionSpec as P

VERY_NEGATIVE = -1e30
LANES = 128
MIB = 1 << 20
AXIS = "ctx"

ROW_A, ROW_SEND_P, ROW_SEND_S, ROW_OWN_P, ROW_OWN_S, ROW_FIN_P, ROW_FIN_K, ROW_FIN_R, ROW_CHAIN = range(9)


class Order:
    def __init__(self):
        self.last = None


def call(order, kernel, operands, outs, name, mib=8, scratch=(), aliases=None, flops=1e6, moved=1e6):
    in_specs, arrays = [], []
    count = len(operands)
    if order.last is not None:
        operands = [*operands, order.last]
    body = lambda *refs: kernel(*refs[:count], *refs[len(operands) :])
    for operand in operands:
        if isinstance(operand, tuple):
            in_specs.append(pl.BlockSpec(memory_space=pl.ANY))
            arrays.append(pltpu.with_memory_space_constraint(operand[0], pltpu.HBM))
        else:
            in_specs.append(pl.BlockSpec(memory_space=pltpu.VMEM))
            arrays.append(pltpu.with_memory_space_constraint(operand, pltpu.VMEM))
    out_specs = [
        pl.BlockSpec(memory_space=pl.ANY if out.memory_space == pltpu.HBM else pltpu.VMEM) for out in outs
    ]
    results = pl.pallas_call(
        body,
        in_specs=in_specs,
        out_specs=out_specs,
        out_shape=list(outs),
        scratch_shapes=list(scratch),
        input_output_aliases=aliases or {},
        compiler_params=pltpu.CompilerParams(vmem_limit_bytes=mib * MIB),
        cost_estimate=pl.CostEstimate(flops=int(flops), bytes_accessed=int(moved), transcendentals=0),
        name=name,
    )(*arrays)
    order.last = results[-1]
    return results


class Operands:
    def __init__(self):
        self.arrays = []

    def place(self, array):
        for i, other in enumerate(self.arrays):
            if other is array:
                return i
        self.arrays.append(array)
        return len(self.arrays) - 1

    def view(self, view):
        return self.place(view[0]), view[1]


def position():
    place = lax.axis_index(AXIS)
    return lax.rem(place, 2), lax.div(place, 2)


def lane_iota(shape):
    return lax.broadcasted_iota(jnp.int32, shape, len(shape) - 1)


def row_iota(shape):
    return lax.broadcasted_iota(jnp.int32, shape, 0)


def lane_order(value, side):
    half = value.shape[0] // 2
    return jnp.where(side == 0, value, jnp.concatenate([value[half:], value[:half]], axis=0))


def head_at(index, heads, side):
    return lax.rem(side * (heads // 2) + index, heads)


def columns_of(head, width):
    return pl.ds(pl.multiple_of(head * width, width), width)


def three_parts(value):
    high = value.astype(jnp.bfloat16).astype(jnp.float32)
    middle = (value - high).astype(jnp.bfloat16).astype(jnp.float32)
    return high, middle, value - high - middle


def memory_of(key, value, weight):
    scaled = (key.astype(jnp.float32) * weight).astype(jnp.bfloat16)
    return lax.dot_general(
        scaled, value, (((0,), (0,)), ((), ())), preferred_element_type=jnp.float32
    )


def start_kernel(
    input_hbm, forget_hbm, keys_hbm, values_hbm,
    keys_ref, rows_ref, columns_ref, summary_ref, first_ref, second_ref,
    input_ref, forget_ref, value_ref, sems,
):
    heads, tokens = input_ref.shape
    dqk = keys_ref.shape[1] // heads
    dv = value_ref.shape[1]
    side, _ = position()
    copies = [
        pltpu.make_async_copy(forget_hbm, forget_ref, sems.at[0]),
        pltpu.make_async_copy(input_hbm, input_ref, sems.at[1]),
    ]
    away = head_at(heads // 2, heads, side)
    copies.append(pltpu.make_async_copy(values_hbm.at[:, columns_of(away, dv)], value_ref, sems.at[2]))
    copies.append(pltpu.make_async_copy(keys_hbm, keys_ref, sems.at[3]))
    for copy in copies:
        copy.start()
    copies[0].wait()
    copies[1].wait()

    gate = lane_order(forget_ref[...], side)
    cumulated = jnp.minimum(gate, 0.0) - jnp.log1p(jnp.exp(-jnp.abs(gate)))
    lanes = lane_iota((heads, tokens))
    step = 1
    while step < tokens:
        cumulated = cumulated + jnp.where(lanes >= step, pltpu.roll(cumulated, step, 1), 0.0)
        step *= 2
    level = lane_order(input_ref[...], side) - cumulated
    running = level
    step = 1
    while step < tokens:
        running = jnp.maximum(
            running, jnp.where(lanes >= step, pltpu.roll(running, step, 1), VERY_NEGATIVE)
        )
        step *= 2
    highest = running[:, tokens - 1 : tokens]
    decay = cumulated[:, tokens - 1 : tokens]
    weight = jnp.exp(level - highest)
    rows_ref[...] = level
    filler = jnp.zeros((LANES - 3 * heads, tokens), jnp.float32)
    columns_ref[...] = jnp.concatenate([weight, running, cumulated, filler], axis=0).T

    copies[2].wait()
    copies[3].wait()
    place = heads // 2
    memory = memory_of(
        keys_ref[:, columns_of(away, dqk)], value_ref[...], columns_ref[:, place : place + 1]
    )
    first_ref[...] = memory[:, : dv // 2]
    second_ref[...] = memory[:, dv // 2 :]

    spare = jnp.zeros((-(-3 * heads // 16) * 16 - 3 * heads, tokens), jnp.float32)
    parts = jnp.concatenate([*three_parts(weight), spare], axis=0).astype(jnp.bfloat16)
    sums = []
    for i in range(heads):
        product = jnp.dot(
            parts, keys_ref[:, columns_of(head_at(i, heads, side), dqk)], preferred_element_type=jnp.float32
        )
        sums.append(
            product[i : i + 1] + product[heads + i : heads + i + 1] + product[2 * heads + i : 2 * heads + i + 1]
        )
    lane = lane_iota((heads, LANES))
    stats = jnp.where(lane == 0, decay + highest, jnp.where(lane == 1, decay, 0.0))
    summary = jnp.concatenate([jnp.concatenate(sums, axis=0), stats], axis=1)
    summary_ref[...] = lane_order(summary, side)


def start(order, input_gate, forget_gate, keys, values):
    heads, tokens = input_gate.shape
    dqk, dv = keys.shape[1] // heads, values.shape[1] // heads
    return call(
        order,
        start_kernel,
        [(a, pl.ANY) for a in (input_gate, forget_gate, keys, values)],
        [
            pltpu.VMEM(keys.shape, keys.dtype),
            pltpu.VMEM((heads, tokens), jnp.float32),
            pltpu.VMEM((tokens, LANES), jnp.float32),
            pltpu.VMEM((heads, dqk + LANES), jnp.float32),
            pltpu.VMEM((dqk, dv // 2), jnp.float32),
            pltpu.VMEM((dqk, dv // 2), jnp.float32),
        ],
        "start",
        mib=12,
        scratch=[
            pltpu.VMEM((heads, tokens), jnp.float32),
            pltpu.VMEM((heads, tokens), jnp.float32),
            pltpu.VMEM((tokens, dv), values.dtype),
            pltpu.SemaphoreType.DMA((4,)),
        ],
        flops=4e9,
        moved=8e6,
    )


def load_kernel(keys_ref, columns_ref, big_hbm, big_ref, *refs, heads, indices):
    *memory_refs, sems = refs
    side, _ = position()
    width = big_ref.shape[1] // heads
    dqk = keys_ref.shape[1] // heads
    order = list(indices) + [i for i in range(heads) if i not in indices]
    copies = {}
    for i in order:
        columns = columns_of(head_at(i, heads, side), width)
        copies[i] = pltpu.make_async_copy(big_hbm.at[:, columns], big_ref.at[:, columns], sems.at[i])
        copies[i].start()
    for i, memory_ref in zip(indices, memory_refs):
        head = head_at(i, heads, side)
        copies[i].wait()
        memory_ref[...] = memory_of(
            keys_ref[:, columns_of(head, dqk)], big_ref[:, columns_of(head, width)], columns_ref[:, i : i + 1]
        )
    for i in order[len(indices) :]:
        copies[i].wait()


def load(order, keys, columns, values, indices, heads):
    tokens = keys.shape[0]
    dqk, dv = keys.shape[1] // heads, values.shape[1] // heads
    outs = call(
        order,
        functools.partial(load_kernel, heads=heads, indices=indices),
        [keys, columns, (values, pl.ANY)],
        [pltpu.VMEM(values.shape, values.dtype)] + [pltpu.VMEM((dqk, dv), jnp.float32)] * len(indices),
        "memories_away",
        mib=12,
        scratch=[pltpu.SemaphoreType.DMA((heads,))],
        flops=4 * len(indices) * tokens * dqk * dv,
        moved=8e6,
    )
    return outs[0], outs[1:]


def memories_kernel(keys_ref, columns_ref, values_ref, queries_hbm, queries_ref, *refs, heads, indices):
    *memory_refs, sem = refs
    side, _ = position()
    dqk, dv = keys_ref.shape[1] // heads, values_ref.shape[1] // heads
    copy = pltpu.make_async_copy(queries_hbm, queries_ref, sem)
    copy.start()
    for i, memory_ref in zip(indices, memory_refs):
        head = head_at(i, heads, side)
        memory_ref[...] = memory_of(
            keys_ref[:, columns_of(head, dqk)], values_ref[:, columns_of(head, dv)], columns_ref[:, i : i + 1]
        )
    copy.wait()


def memories(order, keys, columns, values, queries, indices, heads):
    tokens = keys.shape[0]
    dqk, dv = keys.shape[1] // heads, values.shape[1] // heads
    outs = call(
        order,
        functools.partial(memories_kernel, heads=heads, indices=indices),
        [keys, columns, values, (queries, pl.ANY)],
        [pltpu.VMEM(queries.shape, queries.dtype)] + [pltpu.VMEM((dqk, dv), jnp.float32)] * len(indices),
        "memories_more",
        mib=12,
        scratch=[pltpu.SemaphoreType.DMA],
        flops=4 * len(indices) * tokens * dqk * dv,
        moved=4e6,
    )
    return outs[0], outs[1:]


def own_kernel(keys_ref, columns_ref, values_ref, *memory_refs, heads, indices):
    side, _ = position()
    dqk, dv = keys_ref.shape[1] // heads, values_ref.shape[1] // heads
    for i, memory_ref in zip(indices, memory_refs):
        head = head_at(i, heads, side)
        memory_ref[...] = memory_of(
            keys_ref[:, columns_of(head, dqk)], values_ref[:, columns_of(head, dv)], columns_ref[:, i : i + 1]
        )


def own_memories(order, keys, columns, values, indices, heads):
    tokens = keys.shape[0]
    dqk, dv = keys.shape[1] // heads, values.shape[1] // heads
    return call(
        order,
        functools.partial(own_kernel, heads=heads, indices=indices),
        [keys, columns, values],
        [pltpu.VMEM((dqk, dv), jnp.float32)] * len(indices),
        "memories_own",
        mib=12,
        flops=4 * len(indices) * tokens * dqk * dv,
        moved=4e6,
    )


def weights_kernel(gathered_ref, table_ref, parts_ref, top_row_ref):
    blocks, heads, width = gathered_ref.shape
    dqk = width - LANES
    lane_heads = heads // 2
    levels = blocks // 2
    place = lax.axis_index(AXIS)
    side, level = position()

    tops, decays, normals = [], [], []
    for block in range(blocks):
        held = gathered_ref[lax.rem(block - place + blocks, blocks)]
        normals.append(held[:, :dqk])
        tops.append(held[:, dqk : dqk + 1])
        decays.append(held[:, dqk + 1 : dqk + 2])

    pick = lambda at, value, otherwise: jnp.where(level == at, value, otherwise)
    top = jnp.full((heads, 1), VERY_NEGATIVE, jnp.float32)
    normal = jnp.zeros((heads, dqk), jnp.float32)
    zero = jnp.zeros((heads, 1), jnp.float32)
    mine_a = mine_b = mine_first = mine_second = zero
    carry_p = carry_s = zero
    prefix_top, prefix_normal = zero, normal
    scales = []
    for z in range(levels):
        t0, t1, d0, d1 = tops[2 * z], tops[2 * z + 1], decays[2 * z], decays[2 * z + 1]
        pair_top = jnp.maximum(t0 + d1, t1)
        first, second = jnp.exp(t0 + d1 - pair_top), jnp.exp(t1 - pair_top)
        pair_normal = normals[2 * z] * first + normals[2 * z + 1] * second
        middle_top = jnp.maximum(top + d0, t0)
        alpha, beta = jnp.exp(top + d0 - middle_top), jnp.exp(t0 - middle_top)
        middle_normal = normal * alpha + normals[2 * z] * beta
        pair_decay = d0 + d1
        next_top = jnp.maximum(top + pair_decay, pair_top)
        a, b = jnp.exp(top + pair_decay - next_top), jnp.exp(pair_top - next_top)
        mine_a, mine_b = pick(z, a, mine_a), pick(z, b, mine_b)
        mine_first, mine_second = pick(z, first, mine_first), pick(z, second, mine_second)
        carry_p, carry_s = pick(z, alpha, carry_p), pick(z, beta, carry_s)
        prefix_top = pick(z, jnp.where(side == 0, top, middle_top), prefix_top)
        prefix_normal = pick(z, jnp.where(side == 0, normal, middle_normal), prefix_normal)
        normal = normal * a + pair_normal * b
        top = next_top
        scales.append((a, b))
    later = jnp.ones((heads, 1), jnp.float32)
    final_p = final_l = zero
    for z in reversed(range(levels)):
        a, b = scales[z]
        final_l = pick(z, b * later, final_l)
        later = later * a
        final_p = pick(z, later, final_p)

    one = jnp.ones((heads, 1), jnp.float32)
    by_side = lambda zero_value, one_value: jnp.where(side == 0, zero_value, one_value)
    lanes = lane_iota((heads, LANES))
    rows = row_iota((heads, LANES))
    head_of_chunk = lane_heads * side + lax.div(lanes, 2)
    head_of_step = lane_heads * side + lax.div(jnp.clip(lanes - level, 0, 2 * lane_heads - 1), 2)

    def spread(column, heads_wanted):
        return jnp.sum(jnp.where(rows == heads_wanted, column, 0.0), axis=0, keepdims=True)

    mine_own = by_side(mine_first, mine_second)
    mine_partner = by_side(mine_second, mine_first)
    chain_own = spread(mine_b * mine_own, head_of_step)
    chain_partner = spread(mine_b * mine_partner, head_of_step)
    entries = [
        spread(mine_a, head_of_step),
        spread(by_side(carry_p, one), head_of_chunk),
        spread(by_side(carry_s, zero), head_of_chunk),
        spread(by_side(one, carry_p), head_of_chunk),
        spread(by_side(zero, carry_s), head_of_chunk),
        spread(final_p, head_of_chunk),
        spread(final_l * mine_own, head_of_chunk),
        spread(final_l * mine_partner, head_of_chunk),
    ]
    for z in range(levels):
        entries += [pick(z, chain_own, 0.0), pick(z, chain_partner, 0.0)]
    here = jnp.ones((1, LANES), jnp.float32)
    entries += [pick(z, here, 0.0) for z in range(levels)]
    empty = jnp.zeros((1, LANES), jnp.float32)
    entries += [empty] * (table_ref.shape[0] - len(entries))
    table_ref[...] = jnp.concatenate(entries, axis=0)

    filler = jnp.zeros((LANES - 3 * heads, dqk), jnp.float32)
    parts = jnp.concatenate([*three_parts(lane_order(prefix_normal, side)), filler], axis=0)
    parts_ref[...] = parts.T
    prefix_top = lane_order(jnp.broadcast_to(prefix_top, (heads, LANES)), side)
    filler = jnp.zeros((LANES - heads, LANES), jnp.float32)
    top_row_ref[...] = jnp.concatenate([prefix_top, filler], axis=0).T[:8]


def weights(order, gathered):
    blocks, heads, width = gathered.shape
    dqk = width - LANES
    table_rows = -(-(ROW_CHAIN + 3 * (blocks // 2)) // 8) * 8
    return call(
        order,
        weights_kernel,
        [gathered],
        [
            pltpu.VMEM((table_rows, LANES), jnp.float32),
            pltpu.VMEM((dqk, LANES), jnp.float32),
            pltpu.VMEM((8, LANES), jnp.float32),
        ],
        "weights",
    )


def finals_kernel(gathered_ref, normal_ref, tops_ref):
    blocks, heads, width = gathered_ref.shape
    dqk = width - LANES
    place = lax.axis_index(AXIS)
    top = jnp.full((heads, 1), VERY_NEGATIVE, jnp.float32)
    normal = jnp.zeros((heads, dqk), jnp.float32)
    for block in range(blocks):
        held = gathered_ref[lax.rem(block - place + blocks, blocks)]
        block_top, decay = held[:, dqk : dqk + 1], held[:, dqk + 1 : dqk + 2]
        next_top = jnp.maximum(top + decay, block_top)
        normal = normal * jnp.exp(top + decay - next_top) + held[:, :dqk] * jnp.exp(block_top - next_top)
        top = next_top
    normal_ref[...] = normal
    tops_ref[...] = jnp.where(lane_iota((heads, LANES)) == 0, top, 0.0)


def finals(order, gathered):
    _, heads, width = gathered.shape
    return call(
        order,
        finals_kernel,
        [gathered],
        [pltpu.VMEM((heads, width - LANES), jnp.float32), pltpu.VMEM((heads, LANES), jnp.float32)],
        "finals",
    )


def attention_kernel(
    queries_ref, keys_ref, values_ref, rows_ref, columns_ref, parts_ref, *refs, heads, index
):
    out_ref, sums_ref, products_ref = refs[-3:]
    side, _ = position()
    head = head_at(index, heads, side)
    tokens = queries_ref.shape[0]
    dqk, dv = queries_ref.shape[1] // heads, values_ref.shape[1] // heads
    key_columns, value_columns = columns_of(head, dqk), columns_of(head, dv)
    tile = min(256, tokens)
    level = rows_ref[index : index + 1, :]
    causal = row_iota((tile, tile)) >= lane_iota((tile, tile))
    part_lanes = lane_iota(parts_ref.shape)
    mine = (lax.rem(part_lanes, heads) == index) & (part_lanes < 3 * heads)
    parts = jnp.where(mine, parts_ref[...], 0.0).astype(jnp.bfloat16)

    for begin in range(0, tokens, tile):
        end = begin + tile
        here = pl.ds(begin, tile)
        query = queries_ref[here, key_columns]
        running = columns_ref[here, heads + index : heads + index + 1]
        total = jnp.zeros((tile, 1), jnp.float32)
        result = None
        for low in range(0, end, tile):
            there = pl.ds(low, tile)
            scores = lax.dot_general(
                query, keys_ref[there, key_columns], (((1,), (1,)), ((), ())), preferred_element_type=jnp.float32
            )
            attn = jnp.exp(level[:, low : low + tile] - running) * scores
            if low == begin:
                attn = jnp.where(causal, attn, 0.0)
            total = total + jnp.sum(attn, axis=1, keepdims=True)
            term = jnp.dot(
                attn.astype(jnp.bfloat16), values_ref[there, value_columns], preferred_element_type=jnp.float32
            )
            result = term if result is None else result + term
        product = jnp.dot(query, parts, preferred_element_type=jnp.float32)
        lanes = lane_iota((tile, LANES))
        if len(refs) > 3:
            sums_ref[here, :] = jnp.where(lanes == index, total, refs[0][here, :])
            products_ref[here, :] = refs[1][here, :] + product
        else:
            sums_ref[here, :] = jnp.where(lanes == index, total, 0.0)
            products_ref[here, :] = product
        out_ref[here, :] = result.astype(jnp.bfloat16)


def attention(order, index, queries, keys, values, rows, columns, parts, state):
    tokens = queries.shape[0]
    heads = rows.shape[0]
    dqk, dv = queries.shape[1] // heads, values.shape[1] // heads
    return call(
        order,
        functools.partial(attention_kernel, heads=heads, index=index),
        [queries, keys, values, rows, columns, parts, *state],
        [
            pltpu.VMEM((tokens, dv), jnp.bfloat16),
            pltpu.VMEM((tokens, LANES), jnp.float32),
            pltpu.VMEM((tokens, LANES), jnp.float32),
        ],
        "attention",
        mib=12,
        flops=2 * tokens * tokens * (dqk + dv) * 1.5,
    )


def factors_kernel(columns_ref, top_ref, sums_ref, products_ref, out_ref, *, heads, dqk):
    tokens = columns_ref.shape[0]
    tile = min(256, tokens)
    shift = lambda block, by: pltpu.roll(block, (LANES - by) % LANES, 1)
    for begin in range(0, tokens, tile):
        here = pl.ds(begin, tile)
        product = products_ref[here, :]
        product = product + shift(product, heads) + shift(product, 2 * heads)
        column = columns_ref[here, :]
        running, cumulated = shift(column, heads), shift(column, 2 * heads)
        top = top_ref[0:1, :]
        highest = jnp.maximum(running, top)
        scaling = float(dqk) ** -0.5
        local, carried = jnp.exp(running - highest), jnp.exp(top - highest)
        denominator = (local * sums_ref[here, :] + carried * product) * scaling
        divisor = jnp.maximum(jnp.abs(denominator), jnp.exp(-(cumulated + highest)))
        inverse = scaling / divisor
        out_ref[here, :] = jnp.where(
            lane_iota((tile, LANES)) < heads, local * inverse, pltpu.roll(carried * inverse, heads, 1)
        )


def factors(order, columns, top_row, sums, products, heads, dqk):
    return call(
        order,
        functools.partial(factors_kernel, heads=heads, dqk=dqk),
        [columns, top_row, sums, products],
        [pltpu.VMEM(columns.shape, jnp.float32)],
        "factors",
    )[0]


def finish_kernel(queries_ref, factors_ref, *refs, items, heads):
    arrays = refs[: 2 * len(items)]
    *_, out_hbm, token_ref, scratch, sems = refs
    token_ref[...] = jnp.zeros_like(token_ref)
    side, _ = position()
    tokens = queries_ref.shape[0]
    dqk = queries_ref.shape[1] // heads
    tile = min(256, tokens)
    copies = []
    for place, (index, column) in enumerate(items):
        held_ref, memory_ref = arrays[2 * place : 2 * place + 2]
        dv, width = held_ref.shape[1], memory_ref.shape[1]
        head = head_at(index, heads, side)
        memory = memory_ref[...].astype(jnp.bfloat16)
        target = pl.ds(pl.multiple_of(head * dv + column, width), width)
        for begin in range(0, tokens, tile):
            here = pl.ds(begin, tile)
            local = factors_ref[here, index : index + 1]
            carried = factors_ref[here, heads + index : heads + index + 1]
            term = jnp.dot(
                queries_ref[here, columns_of(head, dqk)], memory, preferred_element_type=jnp.float32
            )
            held = held_ref[here, column : column + width].astype(jnp.float32)
            scratch[place, here, :] = (held * local + term * carried).astype(scratch.dtype)
            copy = pltpu.make_async_copy(
                scratch.at[place, here, :], out_hbm.at[here, target], sems.at[len(copies)]
            )
            copy.start()
            copies.append(copy)
    for copy in copies:
        copy.wait()


def finish(order, items, queries, factor, hidden, heads):
    tokens = queries.shape[0]
    dqk = queries.shape[1] // heads
    dv = items[0][2].shape[1]
    width = items[0][3].shape[1]
    operands = [queries, factor]
    for _, _, held, memory in items:
        operands += [held, memory]
    aliases = {}
    if hidden is not None:
        aliases = {len(operands): 0}
        operands.append((hidden, pl.ANY))
    return call(
        order,
        functools.partial(finish_kernel, items=[item[:2] for item in items], heads=heads),
        operands,
        [pltpu.HBM((tokens, heads * dv), jnp.bfloat16), pltpu.VMEM((8, LANES), jnp.float32)],
        "finish",
        mib=12,
        scratch=[
            pltpu.VMEM((len(items), tokens, width), jnp.bfloat16),
            pltpu.SemaphoreType.DMA((len(items) * max(1, tokens // 256),)),
        ],
        aliases=aliases,
        flops=4 * len(items) * tokens * dqk * width,
    )[0]


def entry_of(table_ref):
    return lambda row, lane: table_ref[row : row + 1, lane : lane + 1]


def row_tiles(rows):
    tile = min(32, rows)
    return [pl.ds(begin, tile) for begin in range(0, rows, tile)]


def chain_kernel(table_ref, *refs, step, views, earlier):
    out_ref = refs[-1]
    half = out_ref.shape[1]
    entry = entry_of(table_ref)
    terms = [(0, 0, entry(ROW_A, step))] if earlier else []
    terms += [(place, column, entry(row, step)) for place, column, row in views]
    for here in row_tiles(out_ref.shape[0]):
        total = None
        for place, column, weight in terms:
            term = refs[place][here, column : column + half] * weight
            total = term if total is None else total + term
        out_ref[here, :] = total


def chain_step(order, table, step, kept, received, earlier, levels, half):
    operands = Operands()
    if earlier is not None:
        operands.place(earlier)
    views = []
    for z in range(levels - 1):
        chunk = step - z
        if 0 <= chunk < len(kept):
            views.append((*operands.view(kept[chunk]), ROW_CHAIN + 2 * z))
            views.append((*operands.view(received[chunk]), ROW_CHAIN + 2 * z + 1))
    return call(
        order,
        functools.partial(chain_kernel, step=step, views=views, earlier=earlier is not None),
        [table, *operands.arrays],
        [pltpu.VMEM((kept[0][0].shape[0], half), jnp.float32)],
        "chain",
    )[0]


def prefix_kernel(table_ref, *refs, levels, pieces):
    send_ref, own_ref = refs[-2:]
    half = send_ref.shape[1] // len(pieces)
    entry = entry_of(table_ref)
    here_row = ROW_CHAIN + 2 * levels
    for i, (chunk, arrivals, (keep, keep_column), (take, take_column)) in enumerate(pieces):
        columns = pl.ds(i * half, half)
        picks = [entry(here_row + z, 0) for z in range(1, levels)]
        send_p, send_s = entry(ROW_SEND_P, chunk), entry(ROW_SEND_S, chunk)
        own_p, own_s = entry(ROW_OWN_P, chunk), entry(ROW_OWN_S, chunk)
        for here in row_tiles(send_ref.shape[0]):
            prefix = None
            for place, weight in zip(arrivals, picks):
                term = refs[place][here, :] * weight
                prefix = term if prefix is None else prefix + term
            send_ref[here, columns] = prefix * send_p + refs[keep][here, keep_column : keep_column + half] * send_s
            own_ref[here, columns] = prefix * own_p + refs[take][here, take_column : take_column + half] * own_s


def prefixes(order, table, chunks, arrived, kept, received, levels, half):
    operands = Operands()
    pieces = []
    for chunk in chunks:
        arrivals = [operands.place(arrived[chunk + z - 1]) for z in range(1, levels)]
        pieces.append((chunk, arrivals, operands.view(kept[chunk]), operands.view(received[chunk])))
    out = pltpu.VMEM((kept[0][0].shape[0], len(chunks) * half), jnp.float32)
    return call(
        order,
        functools.partial(prefix_kernel, levels=levels, pieces=pieces),
        [table, *operands.arrays],
        [out, out],
        "prefix",
    )


def down_kernel(table_ref, *refs, step, levels, views, earlier):
    out_ref = refs[-1]
    _, rows, half = out_ref.shape
    _, level = position()
    target = jnp.maximum(step - levels + level, 0)
    here = pl.ds(pl.multiple_of(target * rows, rows), rows)
    entry = entry_of(table_ref)
    for c, ((keep, keep_column), (take, take_column)) in enumerate(views):
        value = refs[keep][here, keep_column : keep_column + half] * entry(ROW_FIN_K, c)
        value = value + refs[take][here, take_column : take_column + half] * entry(ROW_FIN_R, c)
        out_ref[c] = value if earlier is None else value + refs[earlier][c]


def down(order, table, step, levels, kept, received, earlier, rows, half):
    operands = Operands()
    views = [(operands.view(keep), operands.view(take)) for keep, take in zip(kept, received)]
    place = None if earlier is None else operands.place(earlier)
    return call(
        order,
        functools.partial(down_kernel, step=step, levels=levels, views=views, earlier=place),
        [table, *operands.arrays],
        [pltpu.VMEM((len(kept), rows, half), jnp.float32)],
        "down",
    )[0]


def final_kernel(table_ref, *refs, views, own_views):
    above_ref, keep_out, send_out = refs[-3:]
    _, rows, half = above_ref.shape
    side, level = position()
    here = pl.ds(pl.multiple_of(level * rows, rows), rows)
    entry = entry_of(table_ref)
    share = rows // 2
    for c, ((keep, keep_column), (take, take_column)) in enumerate(views):
        own, send, column = own_views[c]
        prefix = jnp.where(
            side == 0, refs[own][here, column : column + half], refs[send][here, column : column + half]
        )
        value = (
            prefix * entry(ROW_FIN_P, c)
            + refs[keep][here, keep_column : keep_column + half] * entry(ROW_FIN_K, c)
            + refs[take][here, take_column : take_column + half] * entry(ROW_FIN_R, c)
            + above_ref[c]
        )
        low, high = value[:share], value[share:]
        columns = pl.ds((c % 2) * half, half)
        keep_out[c // 2, :, columns] = jnp.where(side == 0, low, high)
        send_out[c // 2, :, columns] = jnp.where(side == 0, high, low)


def final_rows(order, table, kept, received, owns, sends, above):
    operands = Operands()
    views = [(operands.view(keep), operands.view(take)) for keep, take in zip(kept, received)]
    own_views = [
        (operands.place(own[0]), operands.place(sent[0]), own[1]) for own, sent in zip(owns, sends)
    ]
    chunks, rows, half = above.shape
    out = pltpu.VMEM((chunks // 2, rows // 2, 2 * half), jnp.float32)
    return call(
        order,
        functools.partial(final_kernel, views=views, own_views=own_views),
        [table, *operands.arrays, above],
        [out, out],
        "final_rows",
    )


def shards(queries, keys, values, input_gate, forget_gate, *, blocks):
    heads = input_gate.shape[0]
    dqk, dv = queries.shape[1] // heads, values.shape[1] // heads
    half = dv // 2
    lane_heads = heads // 2
    levels = blocks // 2
    chunks = 2 * lane_heads
    place = lax.axis_index(AXIS)
    side = lax.rem(place, 2)
    across = [(i, i ^ 1) for i in range(blocks)]
    up = [(i, i + 2) for i in range(blocks - 2)]
    downward = [(i + 2, i) for i in range(blocks - 2)]
    send = lambda value, pairs: lax.ppermute(value, AXIS, pairs)
    order = Order()

    def views_of(arrays):
        return [(array, column) for array in arrays for column in range(0, array.shape[1], half)]

    keys, rows, columns, summary, *away = start(order, input_gate, forget_gate, keys, values)
    gathered = summary[None]
    received = [send(a, across) for a in away]
    values, (first_away, first_kept) = load(order, keys, columns, values, [lane_heads + 1, 0], heads)
    received.append(send(first_away, across))
    queries, away = memories(
        order, keys, columns, values, queries, range(lane_heads + 2, heads), heads
    )
    received = views_of([*received, *[send(a, across) for a in away]])

    while gathered.shape[0] < blocks:
        reach = gathered.shape[0]
        more = send(gathered, [(i, (i - reach) % blocks) for i in range(blocks)])
        gathered = jnp.concatenate([gathered, more], axis=0)[:blocks]
    table, parts, top_row = weights(order, gathered)

    steps = chunks + levels - 2
    arrived, kept = [], views_of([first_kept])
    attended, state = [], []
    sends, owns, others = [], [], []
    hidden = factor = above = None
    final_normal = tops = None

    def attend(count):
        nonlocal state
        for _ in range(count):
            if len(attended) < heads:
                result, *state = attention(
                    order, len(attended), queries, keys, values, rows, columns, parts, state
                )
                attended.append(result)

    def exchange():
        done = sum(a.shape[1] for a in owns) // half
        whole = done < chunks - 2
        group = list(range(done, done + (2 if whole else 1)))
        if done < chunks and group[-1] + levels - 2 < len(arrived):
            to_send, own = prefixes(order, table, group, arrived, kept, received, levels, half)
            sends.append(to_send)
            owns.append(own)
            others.append(send(to_send, across))

    def item(memories, base, c):
        head = base + min(c, lane_heads - 1)
        return head, (c // lane_heads) * half, attended[head], memories[c]

    def put(*items):
        nonlocal hidden
        hidden = finish(order, items, queries, factor, hidden, heads)

    finished = [0, 0]

    def put_next(which):
        memories, base = ((owns, 0), (others, lane_heads))[which]
        if finished[which] < min(len(memories), lane_heads - 1):
            put(item(memories, base, finished[which]))
            finished[which] += 1

    downs = 0
    for step in range(steps):
        earlier = arrived[step - 1] if step else None
        arrived.append(
            send(chain_step(order, table, step, kept, received, earlier, levels, half), up)
        )
        if step == 0 and lane_heads > 1:
            kept += views_of(own_memories(order, keys, columns, values, range(1, lane_heads), heads))
            attend(1)
            continue
        attend(2)
        if step == 2:
            final_normal, tops = finals(order, gathered)
        if len(attended) == heads and factor is None:
            factor = factors(order, columns, top_row, *state, heads, dqk)
        if step >= 4:
            arrived_now = arrived.pop()
            exchange()
            arrived.append(arrived_now)
        if step >= 5 and step % 2 == 1 and downs < levels - 1:
            downs += 1
            above = send(
                down(order, table, downs, levels, kept, received, above, dqk // levels, half), downward
            )
        if factor is not None:
            put_next(0)
            if step >= 7:
                put_next(1)
    attend(heads)
    if final_normal is None:
        final_normal, tops = finals(order, gathered)
    if factor is None:
        factor = factors(order, columns, top_row, *state, heads, dqk)
    while sum(a.shape[1] for a in owns) < chunks * half:
        exchange()
    while downs < levels - 1:
        downs += 1
        above = send(
            down(order, table, downs, levels, kept, received, above, dqk // levels, half), downward
        )
    keep_rows, send_rows = final_rows(
        order, table, kept, received, views_of(owns), views_of(sends), above
    )
    other_rows = send(send_rows, across)
    while finished[0] < lane_heads - 1:
        put_next(0)
    put(*[item(owns, 0, c) for c in range(lane_heads - 1, len(owns))])
    while finished[1] < lane_heads - 1:
        put_next(1)
    for c in range(lane_heads - 1, len(others)):
        put(item(others, lane_heads, c))

    final_memory = jnp.where(
        side == 0,
        jnp.concatenate([keep_rows, other_rows], axis=0),
        jnp.concatenate([other_rows, keep_rows], axis=0),
    )
    share = dqk // blocks
    final_normalizer = lax.dynamic_slice_in_dim(final_normal, place * share, share, 1)
    return hidden, final_memory, final_normalizer, tops[:, 0]


def solution(mesh):
    token_spec = P(("seq", "ctx"), None)
    gate_spec = P(None, ("seq", "ctx"))
    return jax.shard_map(
        functools.partial(shards, blocks=mesh.shape["ctx"]),
        mesh=mesh,
        in_specs=(token_spec, token_spec, token_spec, gate_spec, gate_spec),
        out_specs=(token_spec, P("seq", "ctx", None), P("seq", "ctx"), P("seq")),
        check_vma=False,
    )
```

```python
import functools

import jax
import jax.numpy as jnp
from jax import lax
from jax.experimental import pallas as pl
from jax.experimental.pallas import tpu as pltpu
from jax.sharding import PartitionSpec as P

VERY_NEGATIVE = -1e30
LANES = 128
MIB = 1 << 20
AXIS = "ctx"

(
    ROW_A, ROW_SEND_P, ROW_SEND_S, ROW_OWN_P, ROW_OWN_S, ROW_FIN_P, ROW_FIN_K, ROW_FIN_R, ROW_FIN_O, ROW_OUT_K, ROW_CHAIN,
) = range(11)


class Order:
    def __init__(self):
        self.last = None
        self.held = []


def call(order, kernel, operands, outs, name, mib=8, scratch=(), aliases=None, flops=1e6, moved=1e6):
    in_specs, arrays = [], []
    count = len(operands)
    for extra in [order.last, *order.held]:
        if extra is not None and not any(extra is operand for operand in operands):
            operands = [*operands, extra]
    body = lambda *refs: kernel(*refs[:count], *refs[len(operands) :])
    for operand in operands:
        if isinstance(operand, tuple):
            in_specs.append(pl.BlockSpec(memory_space=pl.ANY))
            arrays.append(pltpu.with_memory_space_constraint(operand[0], pltpu.HBM))
        else:
            in_specs.append(pl.BlockSpec(memory_space=pltpu.VMEM))
            arrays.append(pltpu.with_memory_space_constraint(operand, pltpu.VMEM))
    out_specs = [
        pl.BlockSpec(memory_space=pl.ANY if out.memory_space == pltpu.HBM else pltpu.VMEM) for out in outs
    ]
    results = pl.pallas_call(
        body,
        in_specs=in_specs,
        out_specs=out_specs,
        out_shape=list(outs),
        scratch_shapes=list(scratch),
        input_output_aliases=aliases or {},
        compiler_params=pltpu.CompilerParams(vmem_limit_bytes=mib * MIB),
        cost_estimate=pl.CostEstimate(flops=int(flops), bytes_accessed=int(moved), transcendentals=0),
        name=name,
    )(*arrays)
    order.last = results[-1]
    return results


class Operands:
    def __init__(self):
        self.arrays = []

    def place(self, array):
        for i, other in enumerate(self.arrays):
            if other is array:
                return i
        self.arrays.append(array)
        return len(self.arrays) - 1

    def view(self, view):
        return self.place(view[0]), view[1]


def position():
    place = lax.axis_index(AXIS)
    return lax.rem(place, 2), lax.div(place, 2)


def lane_iota(shape):
    return lax.broadcasted_iota(jnp.int32, shape, len(shape) - 1)


def row_iota(shape):
    return lax.broadcasted_iota(jnp.int32, shape, 0)


def lane_order(value, side):
    half = value.shape[0] // 2
    return jnp.where(side == 0, value, jnp.concatenate([value[half:], value[:half]], axis=0))


def head_at(index, heads, side):
    return lax.rem(side * (heads // 2) + index, heads)


def columns_of(head, width):
    return pl.ds(pl.multiple_of(head * width, width), width)


def three_parts(value):
    high = value.astype(jnp.bfloat16).astype(jnp.float32)
    middle = (value - high).astype(jnp.bfloat16).astype(jnp.float32)
    return high, middle, value - high - middle


def memory_of(key, value, weight):
    scaled = (key.astype(jnp.float32) * weight).astype(jnp.bfloat16)
    return lax.dot_general(
        scaled, value, (((0,), (0,)), ((), ())), preferred_element_type=jnp.float32
    )


def start_kernel(
    input_hbm, forget_hbm, keys_hbm, values_hbm,
    keys_ref, value_ref, next_ref, rows_ref, columns_ref, summary_ref, input_ref, forget_ref, sems,
):
    heads, tokens = input_ref.shape
    dqk = keys_ref.shape[1] // heads
    dv = value_ref.shape[1]
    side, _ = position()
    away = [head_at(heads // 2 + i, heads, side) for i in range(2)]
    copies = [
        pltpu.make_async_copy(forget_hbm, forget_ref, sems.at[0]),
        pltpu.make_async_copy(input_hbm, input_ref, sems.at[1]),
        pltpu.make_async_copy(keys_hbm, keys_ref, sems.at[2]),
        pltpu.make_async_copy(values_hbm.at[:, columns_of(away[0], dv)], value_ref, sems.at[3]),
        pltpu.make_async_copy(values_hbm.at[:, columns_of(away[1], dv)], next_ref, sems.at[4]),
    ]
    for copy in copies:
        copy.start()
    copies[0].wait()
    copies[1].wait()

    gate = lane_order(forget_ref[...], side)
    cumulated = jnp.minimum(gate, 0.0) - jnp.log1p(jnp.exp(-jnp.abs(gate)))
    lanes = lane_iota((heads, tokens))
    step = 1
    while step < tokens:
        cumulated = cumulated + jnp.where(lanes >= step, pltpu.roll(cumulated, step, 1), 0.0)
        step *= 2
    level = lane_order(input_ref[...], side) - cumulated
    running = level
    step = 1
    while step < tokens:
        running = jnp.maximum(
            running, jnp.where(lanes >= step, pltpu.roll(running, step, 1), VERY_NEGATIVE)
        )
        step *= 2
    highest = running[:, tokens - 1 : tokens]
    decay = cumulated[:, tokens - 1 : tokens]
    weight = jnp.exp(level - highest)
    rows_ref[...] = level
    filler = jnp.zeros((LANES - 3 * heads, tokens), jnp.float32)
    columns_ref[...] = jnp.concatenate([weight, running, cumulated, filler], axis=0).T

    copies[2].wait()
    spare = jnp.zeros((-(-3 * heads // 16) * 16 - 3 * heads, tokens), jnp.float32)
    parts = jnp.concatenate([*three_parts(weight), spare], axis=0).astype(jnp.bfloat16)
    sums = []
    for i in range(heads):
        product = jnp.dot(
            parts, keys_ref[:, columns_of(head_at(i, heads, side), dqk)], preferred_element_type=jnp.float32
        )
        sums.append(
            product[i : i + 1] + product[heads + i : heads + i + 1] + product[2 * heads + i : 2 * heads + i + 1]
        )
    lane = lane_iota((heads, LANES))
    stats = jnp.where(lane == 0, decay + highest, jnp.where(lane == 1, decay, 0.0))
    summary = jnp.concatenate([jnp.concatenate(sums, axis=0), stats], axis=1)
    summary_ref[...] = lane_order(summary, side)
    copies[3].wait()
    copies[4].wait()


def start(order, input_gate, forget_gate, keys, values):
    heads, tokens = input_gate.shape
    dqk, dv = keys.shape[1] // heads, values.shape[1] // heads
    return call(
        order,
        start_kernel,
        [(a, pl.ANY) for a in (input_gate, forget_gate, keys, values)],
        [
            pltpu.VMEM(keys.shape, keys.dtype),
            pltpu.VMEM((tokens, dv), values.dtype),
            pltpu.VMEM((tokens, dv), values.dtype),
            pltpu.VMEM((heads, tokens), jnp.float32),
            pltpu.VMEM((tokens, LANES), jnp.float32),
            pltpu.VMEM((heads, dqk + LANES), jnp.float32),
        ],
        "start",
        mib=12,
        scratch=[
            pltpu.VMEM((heads, tokens), jnp.float32),
            pltpu.VMEM((heads, tokens), jnp.float32),
            pltpu.SemaphoreType.DMA((5,)),
        ],
        flops=2e9,
        moved=5e6,
    )


def away_kernel(keys_ref, columns_ref, value_ref, *refs, heads, place):
    *before, chunk_ref, rest_ref = refs
    side, _ = position()
    index = heads // 2 + place
    dqk, half = rest_ref.shape
    memory = memory_of(
        keys_ref[:, columns_of(head_at(index, heads, side), dqk)], value_ref[...], columns_ref[:, index : index + 1]
    )
    if before:
        chunk_ref[:, :half] = before[0][...]
    chunk_ref[:, chunk_ref.shape[1] - half :] = memory[:, :half]
    rest_ref[...] = memory[:, half:]


def away_memory(order, place, keys, columns, value, before, heads):
    tokens, dv = value.shape
    dqk = keys.shape[1] // heads
    half = dv // 2
    return call(
        order,
        functools.partial(away_kernel, heads=heads, place=place),
        [keys, columns, value, *before],
        [
            pltpu.VMEM((dqk, half * (1 + len(before))), jnp.float32),
            pltpu.VMEM((dqk, half), jnp.float32),
        ],
        "away_memory",
        mib=12,
        flops=0,
        moved=0,
    )


def load_kernel(keys_ref, columns_ref, big_hbm, big_ref, memory_ref, sems, *, heads):
    side, _ = position()
    width = big_ref.shape[1] // heads
    dqk = keys_ref.shape[1] // heads
    copies = []
    for i in range(heads):
        columns = columns_of(head_at(i, heads, side), width)
        copies.append(pltpu.make_async_copy(big_hbm.at[:, columns], big_ref.at[:, columns], sems.at[i]))
        copies[i].start()
    copies[0].wait()
    head = head_at(0, heads, side)
    memory_ref[...] = memory_of(
        keys_ref[:, columns_of(head, dqk)], big_ref[:, columns_of(head, width)], columns_ref[:, 0:1]
    )
    for copy in copies[1:]:
        copy.wait()


def load(order, keys, columns, values, heads):
    tokens = keys.shape[0]
    dqk, dv = keys.shape[1] // heads, values.shape[1] // heads
    return call(
        order,
        functools.partial(load_kernel, heads=heads),
        [keys, columns, (values, pl.ANY)],
        [pltpu.VMEM(values.shape, values.dtype), pltpu.VMEM((dqk, dv), jnp.float32)],
        "load",
        mib=12,
        scratch=[pltpu.SemaphoreType.DMA((heads,))],
        flops=4 * tokens * dqk * dv,
        moved=8e6,
    )


def memories_kernel(keys_ref, columns_ref, values_ref, queries_hbm, rest_ref, queries_ref, *refs, heads):
    *chunk_refs, sem = refs
    side, _ = position()
    dqk, dv = keys_ref.shape[1] // heads, values_ref.shape[1] // heads
    half = dv // 2
    copy = pltpu.make_async_copy(queries_hbm, queries_ref, sem)
    copy.start()
    rest = rest_ref[...]
    for place, chunk_ref in enumerate(chunk_refs[:-1]):
        index = heads // 2 + 2 + place
        head = head_at(index, heads, side)
        memory = memory_of(
            keys_ref[:, columns_of(head, dqk)], values_ref[:, columns_of(head, dv)], columns_ref[:, index : index + 1]
        )
        chunk_ref[:, :half] = rest
        chunk_ref[:, half:] = memory[:, :half]
        rest = memory[:, half:]
    chunk_refs[-1][...] = rest
    copy.wait()


def memories(order, keys, columns, values, queries, rest, heads):
    tokens = keys.shape[0]
    dqk, dv = keys.shape[1] // heads, values.shape[1] // heads
    count = heads // 2 - 2
    outs = call(
        order,
        functools.partial(memories_kernel, heads=heads),
        [keys, columns, values, (queries, pl.ANY), rest],
        [pltpu.VMEM(queries.shape, queries.dtype)]
        + [pltpu.VMEM((dqk, dv), jnp.float32)] * count
        + [pltpu.VMEM((dqk, dv // 2), jnp.float32)],
        "memories_away",
        mib=12,
        scratch=[pltpu.SemaphoreType.DMA],
        flops=4 * count * tokens * dqk * dv,
        moved=4e6,
    )
    return outs[0], outs[1:]


def own_kernel(keys_ref, columns_ref, values_ref, *memory_refs, heads, indices):
    side, _ = position()
    dqk, dv = keys_ref.shape[1] // heads, values_ref.shape[1] // heads
    for i, memory_ref in zip(indices, memory_refs):
        head = head_at(i, heads, side)
        memory_ref[...] = memory_of(
            keys_ref[:, columns_of(head, dqk)], values_ref[:, columns_of(head, dv)], columns_ref[:, i : i + 1]
        )


def own_memories(order, keys, columns, values, indices, heads):
    tokens = keys.shape[0]
    dqk, dv = keys.shape[1] // heads, values.shape[1] // heads
    return call(
        order,
        functools.partial(own_kernel, heads=heads, indices=indices),
        [keys, columns, values],
        [pltpu.VMEM((dqk, dv), jnp.float32)] * len(indices),
        "memories_own",
        mib=12,
        flops=4 * len(indices) * tokens * dqk * dv,
        moved=4e6,
    )


def block_summary(gathered_ref, block, side, level):
    levels = gathered_ref.shape[0]
    turn = lax.rem(block // 2 - level + levels, levels)
    same, other = gathered_ref[turn, 0], gathered_ref[turn, 1]
    return jnp.where(side == block % 2, same, other)


def weights_kernel(gathered_ref, table_ref, parts_ref, top_row_ref):
    levels, _, heads, width = gathered_ref.shape
    blocks = 2 * levels
    dqk = width - LANES
    lane_heads = heads // 2
    side, level = position()

    tops, decays, normals = [], [], []
    for block in range(blocks):
        held = block_summary(gathered_ref, block, side, level)
        normals.append(held[:, :dqk])
        tops.append(held[:, dqk : dqk + 1])
        decays.append(held[:, dqk + 1 : dqk + 2])

    pick = lambda at, value, otherwise: jnp.where(level == at, value, otherwise)
    top = jnp.full((heads, 1), VERY_NEGATIVE, jnp.float32)
    normal = jnp.zeros((heads, dqk), jnp.float32)
    zero = jnp.zeros((heads, 1), jnp.float32)
    mine_a = mine_b = mine_first = mine_second = zero
    carry_p = carry_s = zero
    prefix_top, prefix_normal = zero, normal
    scales = []
    for z in range(levels):
        t0, t1, d0, d1 = tops[2 * z], tops[2 * z + 1], decays[2 * z], decays[2 * z + 1]
        pair_top = jnp.maximum(t0 + d1, t1)
        first, second = jnp.exp(t0 + d1 - pair_top), jnp.exp(t1 - pair_top)
        pair_normal = normals[2 * z] * first + normals[2 * z + 1] * second
        middle_top = jnp.maximum(top + d0, t0)
        alpha, beta = jnp.exp(top + d0 - middle_top), jnp.exp(t0 - middle_top)
        middle_normal = normal * alpha + normals[2 * z] * beta
        pair_decay = d0 + d1
        next_top = jnp.maximum(top + pair_decay, pair_top)
        a, b = jnp.exp(top + pair_decay - next_top), jnp.exp(pair_top - next_top)
        mine_a, mine_b = pick(z, a, mine_a), pick(z, b, mine_b)
        mine_first, mine_second = pick(z, first, mine_first), pick(z, second, mine_second)
        carry_p, carry_s = pick(z, alpha, carry_p), pick(z, beta, carry_s)
        prefix_top = pick(z, jnp.where(side == 0, top, middle_top), prefix_top)
        prefix_normal = pick(z, jnp.where(side == 0, normal, middle_normal), prefix_normal)
        normal = normal * a + pair_normal * b
        top = next_top
        scales.append((a, b, jnp.exp(middle_top + d1 - next_top)))
    later = jnp.ones((heads, 1), jnp.float32)
    final_p = final_l = final_m = zero
    for z in reversed(range(levels)):
        a, b, middle = scales[z]
        final_l = pick(z, b * later, final_l)
        final_m = pick(z, middle * later, final_m)
        later = later * a
        final_p = pick(z, later, final_p)

    one = jnp.ones((heads, 1), jnp.float32)
    by_side = lambda zero_value, one_value: jnp.where(side == 0, zero_value, one_value)
    lanes = lane_iota((heads, LANES))
    rows = row_iota((heads, LANES))
    head_of_unit = lane_heads * side + lax.div(lanes, 2)
    other_of_unit = lane_heads * (1 - side) + lax.div(lanes, 2)
    head_of_step = lane_heads * side + lax.div(jnp.clip(lanes - 2 * level - 1, 0, 2 * lane_heads - 1), 2)

    def spread(column, heads_wanted):
        return jnp.sum(jnp.where(rows == heads_wanted, column, 0.0), axis=0, keepdims=True)

    mine_own = by_side(mine_first, mine_second)
    mine_partner = by_side(mine_second, mine_first)
    chain_own = spread(mine_b * mine_own, head_of_step)
    chain_partner = spread(mine_b * mine_partner, head_of_step)
    entries = [
        spread(mine_a, head_of_step),
        spread(by_side(carry_p, one), head_of_unit),
        spread(by_side(carry_s, zero), head_of_unit),
        spread(by_side(one, carry_p), head_of_unit),
        spread(by_side(zero, carry_s), head_of_unit),
        spread(final_p, head_of_unit),
        spread(final_l * mine_own, head_of_unit),
        spread(final_l * mine_partner, head_of_unit),
        spread(by_side(final_p, final_m), other_of_unit),
        spread(by_side(zero, final_l * mine_own), head_of_unit),
    ]
    for z in range(levels):
        entries += [pick(z, chain_own, 0.0), pick(z, chain_partner, 0.0)]
    here = jnp.ones((1, LANES), jnp.float32)
    entries += [pick(z, here, 0.0) for z in range(levels)]
    empty = jnp.zeros((1, LANES), jnp.float32)
    entries += [empty] * (table_ref.shape[0] - len(entries))
    table_ref[...] = jnp.concatenate(entries, axis=0)

    filler = jnp.zeros((LANES - 3 * heads, dqk), jnp.float32)
    parts = jnp.concatenate([*three_parts(lane_order(prefix_normal, side)), filler], axis=0)
    parts_ref[...] = parts.T
    prefix_top = lane_order(jnp.broadcast_to(prefix_top, (heads, LANES)), side)
    filler = jnp.zeros((LANES - heads, LANES), jnp.float32)
    top_row_ref[...] = jnp.concatenate([prefix_top, filler], axis=0).T[:8]


def weights(order, gathered):
    levels, _, heads, width = gathered.shape
    dqk = width - LANES
    table_rows = -(-(ROW_CHAIN + 3 * levels) // 8) * 8
    return call(
        order,
        weights_kernel,
        [gathered],
        [
            pltpu.VMEM((table_rows, LANES), jnp.float32),
            pltpu.VMEM((dqk, LANES), jnp.float32),
            pltpu.VMEM((8, LANES), jnp.float32),
        ],
        "weights",
    )


def wait_kernel(ref, out_ref):
    out_ref[...] = ref[:8, :LANES]


def wait(order, array):
    return call(order, wait_kernel, [array], [pltpu.VMEM((8, LANES), jnp.float32)], "wait")[0]


def pack_kernel(*refs):
    *in_refs, out_ref = refs
    at = 0
    for ref in in_refs:
        value = ref[...].reshape((-1,) + out_ref.shape[1:])
        count = min(value.shape[0], out_ref.shape[0] - at)
        out_ref[at : at + count] = value[:count]
        at += count


def pack(order, arrays, count):
    shape = arrays[0].shape[-2:] if count == 2 and arrays[0].ndim == 2 else arrays[0].shape[1:]
    return call(order, pack_kernel, arrays, [pltpu.VMEM((count,) + shape, jnp.float32)], "pack")[0]


def finals_kernel(gathered_ref, normal_hbm, tops_hbm, token_ref, normal_ref, tops_ref, sems):
    token_ref[...] = jnp.zeros_like(token_ref)
    levels, _, heads, width = gathered_ref.shape
    dqk = width - LANES
    side, level = position()
    top = jnp.full((heads, 1), VERY_NEGATIVE, jnp.float32)
    normal = jnp.zeros((heads, dqk), jnp.float32)
    for block in range(2 * levels):
        held = block_summary(gathered_ref, block, side, level)
        block_top, decay = held[:, dqk : dqk + 1], held[:, dqk + 1 : dqk + 2]
        next_top = jnp.maximum(top + decay, block_top)
        normal = normal * jnp.exp(top + decay - next_top) + held[:, :dqk] * jnp.exp(block_top - next_top)
        top = next_top
    share = normal_hbm.shape[1]
    place = 2 * level + side
    mine = pltpu.roll(normal, lax.rem(dqk - place * share, dqk), 1)
    normal_ref[...] = mine[:, :share]
    filler = jnp.zeros((LANES - heads, LANES), jnp.float32)
    tops = jnp.concatenate([jnp.broadcast_to(top, (heads, LANES)), filler], axis=0).T
    tops_ref[...] = tops[0:1, :heads]
    copies = [
        pltpu.make_async_copy(normal_ref, normal_hbm, sems.at[0]),
        pltpu.make_async_copy(tops_ref, tops_hbm, sems.at[1]),
    ]
    for copy in copies:
        copy.start()
    for copy in copies:
        copy.wait()


def finals(order, gathered):
    levels, _, heads, width = gathered.shape
    shape = (heads, (width - LANES) // (2 * levels))
    normal, tops, _ = call(
        order,
        finals_kernel,
        [gathered],
        [
            pltpu.HBM(shape, jnp.float32),
            pltpu.HBM((1, heads), jnp.float32),
            pltpu.VMEM((8, LANES), jnp.float32),
        ],
        "finals",
        scratch=[
            pltpu.VMEM(shape, jnp.float32),
            pltpu.VMEM((1, heads), jnp.float32),
            pltpu.SemaphoreType.DMA((2,)),
        ],
    )
    return normal, tops


def attention_kernel(
    queries_ref, keys_ref, values_ref, rows_ref, columns_ref, parts_ref, *refs, heads, index
):
    out_ref, sums_ref, products_ref = refs[-3:]
    side, _ = position()
    head = head_at(index, heads, side)
    tokens = queries_ref.shape[0]
    dqk, dv = queries_ref.shape[1] // heads, values_ref.shape[1] // heads
    key_columns, value_columns = columns_of(head, dqk), columns_of(head, dv)
    tile = min(256, tokens)
    level = rows_ref[index : index + 1, :]
    causal = row_iota((tile, tile)) >= lane_iota((tile, tile))
    part_lanes = lane_iota(parts_ref.shape)
    mine = (lax.rem(part_lanes, heads) == index) & (part_lanes < 3 * heads)
    parts = jnp.where(mine, parts_ref[...], 0.0).astype(jnp.bfloat16)

    for begin in range(0, tokens, tile):
        end = begin + tile
        here = pl.ds(begin, tile)
        query = queries_ref[here, key_columns]
        running = columns_ref[here, heads + index : heads + index + 1]
        total = jnp.zeros((tile, 1), jnp.float32)
        result = None
        for low in range(0, end, tile):
            there = pl.ds(low, tile)
            scores = lax.dot_general(
                query, keys_ref[there, key_columns], (((1,), (1,)), ((), ())), preferred_element_type=jnp.float32
            )
            attn = jnp.exp(level[:, low : low + tile] - running) * scores
            if low == begin:
                attn = jnp.where(causal, attn, 0.0)
            total = total + jnp.sum(attn, axis=1, keepdims=True)
            term = jnp.dot(
                attn.astype(jnp.bfloat16), values_ref[there, value_columns], preferred_element_type=jnp.float32
            )
            result = term if result is None else result + term
        product = jnp.dot(query, parts, preferred_element_type=jnp.float32)
        lanes = lane_iota((tile, LANES))
        if len(refs) > 3:
            sums_ref[here, :] = jnp.where(lanes == index, total, refs[0][here, :])
            products_ref[here, :] = refs[1][here, :] + product
        else:
            sums_ref[here, :] = jnp.where(lanes == index, total, 0.0)
            products_ref[here, :] = product
        out_ref[here, :] = result.astype(jnp.bfloat16)


def attention(order, index, queries, keys, values, rows, columns, parts, state):
    tokens = queries.shape[0]
    heads = rows.shape[0]
    dqk, dv = queries.shape[1] // heads, values.shape[1] // heads
    return call(
        order,
        functools.partial(attention_kernel, heads=heads, index=index),
        [queries, keys, values, rows, columns, parts, *state],
        [
            pltpu.VMEM((tokens, dv), jnp.bfloat16),
            pltpu.VMEM((tokens, LANES), jnp.float32),
            pltpu.VMEM((tokens, LANES), jnp.float32),
        ],
        "attention",
        mib=12,
        flops=2 * tokens * tokens * (dqk + dv) * 1.5,
    )


def factors_kernel(columns_ref, top_ref, sums_ref, products_ref, out_ref, *, heads, dqk):
    tokens = columns_ref.shape[0]
    tile = min(256, tokens)
    shift = lambda block, by: pltpu.roll(block, (LANES - by) % LANES, 1)
    for begin in range(0, tokens, tile):
        here = pl.ds(begin, tile)
        product = products_ref[here, :]
        product = product + shift(product, heads) + shift(product, 2 * heads)
        column = columns_ref[here, :]
        running, cumulated = shift(column, heads), shift(column, 2 * heads)
        top = top_ref[0:1, :]
        highest = jnp.maximum(running, top)
        scaling = float(dqk) ** -0.5
        local, carried = jnp.exp(running - highest), jnp.exp(top - highest)
        denominator = (local * sums_ref[here, :] + carried * product) * scaling
        divisor = jnp.maximum(jnp.abs(denominator), jnp.exp(-(cumulated + highest)))
        inverse = scaling / divisor
        out_ref[here, :] = jnp.where(
            lane_iota((tile, LANES)) < heads, local * inverse, pltpu.roll(carried * inverse, heads, 1)
        )


def factors(order, columns, top_row, sums, products, heads, dqk):
    return call(
        order,
        functools.partial(factors_kernel, heads=heads, dqk=dqk),
        [columns, top_row, sums, products],
        [pltpu.VMEM(columns.shape, jnp.float32)],
        "factors",
    )[0]


def finish_units(queries_ref, factors_ref, refs, items, heads, out_hbm, scratch, sems):
    side, _ = position()
    tokens = queries_ref.shape[0]
    dqk = queries_ref.shape[1] // heads
    half = scratch.shape[2]
    tile = min(256, tokens)
    copies = []
    for at, (index, which, held, place, column) in enumerate(items):
        head = head_at(index, heads, side)
        memory = refs[place][:, column : column + half].astype(jnp.bfloat16)
        target = pl.ds(pl.multiple_of((2 * head + which) * half, half), half)
        for begin in range(0, tokens, tile):
            here = pl.ds(begin, tile)
            local = factors_ref[here, index : index + 1]
            carried = factors_ref[here, heads + index : heads + index + 1]
            term = jnp.dot(
                queries_ref[here, columns_of(head, dqk)], memory, preferred_element_type=jnp.float32
            )
            value = refs[held][here, which * half : (which + 1) * half].astype(jnp.float32)
            scratch[at, here, :] = (value * local + term * carried).astype(scratch.dtype)
            copy = pltpu.make_async_copy(
                scratch.at[at, here, :], out_hbm.at[here, target], sems.at[len(copies)]
            )
            copy.start()
            copies.append(copy)
    return copies


def finish_kernel(queries_ref, factors_ref, *refs, items, heads):
    *_, out_hbm, token_ref, scratch, sems = refs
    token_ref[...] = jnp.zeros_like(token_ref)
    for copy in finish_units(queries_ref, factors_ref, refs, items, heads, out_hbm, scratch, sems):
        copy.wait()


def finish_operands(units):
    operands = Operands()
    items = [
        (index, which, operands.place(held), *operands.view(view)) for index, which, held, view in units
    ]
    return operands, items


def finish_scratch(units, tokens):
    half = units[0][2].shape[1] // 2
    return [
        pltpu.VMEM((len(units), tokens, half), jnp.bfloat16),
        pltpu.SemaphoreType.DMA((len(units) * max(1, tokens // 256),)),
    ]


def finish(order, units, queries, factor, hidden, heads):
    operands, items = finish_operands(units)
    tokens = queries.shape[0]
    dv = units[0][2].shape[1]
    arrays = [queries, factor, *operands.arrays]
    aliases = {}
    if hidden is not None:
        aliases = {len(arrays): 0}
        arrays.append((hidden, pl.ANY))
    return call(
        order,
        functools.partial(finish_kernel, items=items, heads=heads),
        arrays,
        [pltpu.HBM((tokens, heads * dv), jnp.bfloat16), pltpu.VMEM((8, LANES), jnp.float32)],
        "finish",
        mib=12,
        scratch=finish_scratch(units, tokens),
        aliases=aliases,
        flops=8e8 * len(units),
    )[0]


def entry_of(table_ref):
    return lambda row, lane: table_ref[row : row + 1, lane : lane + 1]


def row_tiles(rows):
    tile = min(32, rows)
    return [pl.ds(begin, tile) for begin in range(0, rows, tile)]


def chain_kernel(table_ref, *refs, slots, half):
    out_ref = refs[-1]
    entry = entry_of(table_ref)
    for i, terms in enumerate(slots):
        terms = [(place, column, entry(row, lane)) for place, column, row, lane in terms]
        for here in row_tiles(out_ref.shape[0]):
            total = None
            for place, column, weight in terms:
                term = refs[place][here, column : column + half] * weight
                total = term if total is None else total + term
            out_ref[here, i * half : (i + 1) * half] = total


def first_kernel(pair_ref, keep_ref, take_ref, out_ref):
    side, _ = position()
    heads, width = pair_ref.shape[1:]
    half = out_ref.shape[1]
    top, decay = [], []
    for which in range(2):
        low, high = pair_ref[which, 0:1, width - LANES :], pair_ref[which, heads // 2 : heads // 2 + 1, width - LANES :]
        stats = jnp.where(side == 0, low, high)
        top.append(stats[:, 0:1])
        decay.append(stats[:, 1:2])
    own = top[0] + jnp.where(side == 0, decay[1], 0.0)
    partner = top[1] + jnp.where(side == 0, 0.0, decay[0])
    highest = jnp.maximum(own, partner)
    own, partner = jnp.exp(own - highest), jnp.exp(partner - highest)
    for here in row_tiles(out_ref.shape[0]):
        out_ref[here, :] = keep_ref[here, :half] * own + take_ref[here, :half] * partner


def first_step(order, pair, kept, received, half):
    return call(
        order,
        first_kernel,
        [pair, kept[0][0], received[0][0]],
        [pltpu.VMEM((kept[0][0].shape[0], half), jnp.float32)],
        "chain",
    )[0]


def chain_step(order, table, step, kept, received, earlier, levels, half):
    operands = Operands()
    slots, columns = [], {}
    for slot in range(2):
        terms = []
        lane = 2 * step + slot
        for z in range(levels - 1):
            unit = 2 * (step - z) - 1 + slot
            if 0 <= unit < len(kept):
                terms.append((*operands.view(kept[unit]), ROW_CHAIN + 2 * z, lane))
                terms.append((*operands.view(received[unit]), ROW_CHAIN + 2 * z + 1, lane))
        if terms:
            if slot in earlier[1]:
                terms.append((operands.place(earlier[0]), earlier[1][slot], ROW_A, lane))
            columns[slot] = half * len(slots)
            slots.append(terms)
    value = call(
        order,
        functools.partial(chain_kernel, slots=slots, half=half),
        [table, *operands.arrays],
        [pltpu.VMEM((kept[0][0].shape[0], half * len(slots)), jnp.float32)],
        "chain",
    )[0]
    return value, columns


def prefix_kernel(table_ref, *refs, levels, pieces, half):
    send_ref, own_ref = refs[-2:]
    entry = entry_of(table_ref)
    here_row = ROW_CHAIN + 2 * levels
    picks = [entry(here_row + z, 0) for z in range(1, levels)]
    for i, (unit, arrivals, (keep, keep_column), (take, take_column)) in enumerate(pieces):
        columns = pl.ds(i * half, half)
        send_p, send_s = entry(ROW_SEND_P, unit), entry(ROW_SEND_S, unit)
        own_p, own_s = entry(ROW_OWN_P, unit), entry(ROW_OWN_S, unit)
        for here in row_tiles(send_ref.shape[0]):
            prefix = None
            for (place, column), weight in zip(arrivals, picks):
                term = refs[place][here, column : column + half] * weight
                prefix = term if prefix is None else prefix + term
            send_ref[here, columns] = prefix * send_p + refs[keep][here, keep_column : keep_column + half] * send_s
            own_ref[here, columns] = prefix * own_p + refs[take][here, take_column : take_column + half] * own_s


def prefixes(order, table, chunk, arrived, kept, received, levels, half):
    operands = Operands()
    pieces = []
    for unit in (2 * chunk - 1, 2 * chunk):
        if 0 <= unit < len(kept):
            arrivals = []
            for z in range(1, levels):
                array, columns = arrived[chunk + z - 1]
                arrivals.append(operands.view((array, columns[unit - 2 * chunk + 1])))
            pieces.append((unit, arrivals, operands.view(kept[unit]), operands.view(received[unit])))
    out = pltpu.VMEM((kept[0][0].shape[0], len(pieces) * half), jnp.float32)
    return call(
        order,
        functools.partial(prefix_kernel, levels=levels, pieces=pieces, half=half),
        [table, *operands.arrays],
        [out, out],
        "prefix",
    )


def down_kernel(table_ref, *refs, step, levels, views, earlier):
    out_ref = refs[-1]
    _, rows, half = out_ref.shape
    _, level = position()
    target = jnp.maximum(step - levels + level, 0)
    here = pl.ds(pl.multiple_of(target * rows, rows), rows)
    entry = entry_of(table_ref)
    for c, ((keep, keep_column), (take, take_column)) in enumerate(views):
        value = refs[keep][here, keep_column : keep_column + half] * entry(ROW_FIN_K, c)
        value = value + refs[take][here, take_column : take_column + half] * entry(ROW_FIN_R, c)
        out_ref[c] = value if earlier is None else value + refs[earlier][c]


def down(order, table, step, levels, kept, received, earlier, rows, half):
    operands = Operands()
    views = [(operands.view(keep), operands.view(take)) for keep, take in zip(kept, received)]
    place = None if earlier is None else operands.place(earlier)
    return call(
        order,
        functools.partial(down_kernel, step=step, levels=levels, views=views, earlier=place),
        [table, *operands.arrays],
        [pltpu.VMEM((len(kept), rows, half), jnp.float32)],
        "down",
    )[0]


def outgoing_kernel(table_ref, *refs, views):
    above_ref, out_ref = refs[-2:]
    _, rows, half = above_ref.shape
    side, level = position()
    entry = entry_of(table_ref)
    share = rows // 2
    there = pl.ds(pl.multiple_of((1 - side) * share, share), share)
    here = pl.ds(pl.multiple_of(level * rows + (1 - side) * share, share), share)
    for c, ((keep, keep_column), (take, take_column)) in enumerate(views):
        out_ref[c // 2, :, pl.ds((c % 2) * half, half)] = (
            above_ref[c, there, :]
            + refs[keep][here, keep_column : keep_column + half] * entry(ROW_OUT_K, c)
            + refs[take][here, take_column : take_column + half] * entry(ROW_FIN_R, c)
        )


def outgoing(order, table, kept, received, above):
    operands = Operands()
    views = [(operands.view(keep), operands.view(take)) for keep, take in zip(kept, received)]
    chunks, rows, half = above.shape
    return call(
        order,
        functools.partial(outgoing_kernel, views=views),
        [table, *operands.arrays, above],
        [pltpu.VMEM((chunks // 2, rows // 2, 2 * half), jnp.float32)],
        "outgoing",
    )[0]


def assemble(table_ref, above_ref, partner_ref, refs, out_ref, *, views, prefix_views, other_views):
    _, rows, half = above_ref.shape
    side, level = position()
    entry = entry_of(table_ref)
    share = rows // 2
    lane_heads = len(views) // 2
    there = pl.ds(pl.multiple_of(side * share, share), share)
    here = pl.ds(pl.multiple_of(level * rows + side * share, share), share)
    at = lambda view: refs[view[0]][here, view[1] : view[1] + half]
    for c, (keep, take) in enumerate(views):
        own, sent = prefix_views[c]
        columns = pl.ds((c % 2) * half, half)
        out_ref[lane_heads * side + c // 2, :, columns] = (
            jnp.where(side == 0, at(own), at(sent)) * entry(ROW_FIN_P, c)
            + at(keep) * entry(ROW_FIN_K, c)
            + at(take) * entry(ROW_FIN_R, c)
            + above_ref[c, there, :]
        )
        out_ref[lane_heads * (1 - side) + c // 2, :, columns] = (
            at(other_views[c]) * entry(ROW_FIN_O, c) + partner_ref[c // 2, :, columns]
        )


def last_kernel(queries_ref, factors_ref, table_ref, above_ref, partner_ref, *refs, items, heads, layout):
    out_hbm, final_hbm, token_ref, scratch, sems, final_ref, final_sem = refs[-7:]
    token_ref[...] = jnp.zeros_like(token_ref)
    copies = finish_units(queries_ref, factors_ref, refs, items, heads, out_hbm, scratch, sems)
    assemble(table_ref, above_ref, partner_ref, refs, final_ref, **layout)
    copies.append(pltpu.make_async_copy(final_ref, final_hbm, final_sem))
    copies[-1].start()
    for copy in copies:
        copy.wait()


def last(order, units, queries, factor, hidden, heads, table, above, partner, kept, received, owns, sends, others):
    operands, items = finish_operands(units)
    layout = {
        "views": [(operands.view(keep), operands.view(take)) for keep, take in zip(kept, received)],
        "prefix_views": [(operands.view(own), operands.view(sent)) for own, sent in zip(owns, sends)],
        "other_views": [operands.view(other) for other in others],
    }
    tokens = queries.shape[0]
    dv = units[0][2].shape[1]
    share = above.shape[1] // 2
    arrays = [queries, factor, table, above, partner, *operands.arrays, (hidden, pl.ANY)]
    return call(
        order,
        functools.partial(last_kernel, items=items, heads=heads, layout=layout),
        arrays,
        [
            pltpu.HBM((tokens, heads * dv), jnp.bfloat16),
            pltpu.HBM((heads, share, dv), jnp.float32),
            pltpu.VMEM((8, LANES), jnp.float32),
        ],
        "last",
        mib=12,
        scratch=[
            *finish_scratch(units, tokens),
            pltpu.VMEM((heads, share, dv), jnp.float32),
            pltpu.SemaphoreType.DMA,
        ],
        aliases={len(arrays) - 1: 0},
        flops=1e9,
    )[:2]


def shards(queries, keys, values, input_gate, forget_gate, *, blocks):
    heads = input_gate.shape[0]
    dqk, dv = queries.shape[1] // heads, values.shape[1] // heads
    half = dv // 2
    lane_heads = heads // 2
    levels = blocks // 2
    across = [(i, i ^ 1) for i in range(blocks)]
    up = [(i, i + 2) for i in range(blocks - 2)]
    downward = [(i + 2, i) for i in range(blocks - 2)]
    send = lambda value, pairs: lax.ppermute(value, AXIS, pairs)
    order = Order()

    def views_of(arrays):
        return [(array, column) for array in arrays for column in range(0, array.shape[1], half)]

    keys, value, next_value, rows, columns, summary = start(order, input_gate, forget_gate, keys, values)
    partner_summary = send(summary, across)
    chunk, rest = away_memory(order, 0, keys, columns, value, [], heads)
    taken = [send(chunk, across)]
    pair = pack(order, [summary, partner_summary], 2)
    chunk, rest = away_memory(order, 1, keys, columns, next_value, [rest], heads)
    taken.append(send(chunk, across))

    gathered = pair[None]
    rounds = 0
    while gathered.shape[0] < levels:
        reach = gathered.shape[0]
        more = send(gathered, [(i, (i - 2 * reach) % blocks) for i in range(blocks)])
        if rounds == 0:
            values, first_kept = load(order, keys, columns, values, heads)
            kept = views_of([first_kept])
        if rounds == 1:
            arrived = [(send(first_step(order, pair, kept, views_of(taken), half), up), {1: 0})]
            queries, away = memories(order, keys, columns, values, queries, rest, heads)
            taken += [send(a, across) for a in away]
        gathered = pack(order, [gathered, more], min(2 * reach, levels))
        rounds += 1
    kept += views_of(own_memories(order, keys, columns, values, range(1, 2), heads))
    table, parts, top_row = weights(order, gathered)
    received = views_of(taken)

    units = 2 * lane_heads
    chunks = lane_heads + 1
    steps = chunks + levels - 2
    attended, state = [], ()
    sends, owns, others = [], [], []
    hidden = factor = above = None
    final_normal = tops = None
    falls = 0

    def attend(count):
        nonlocal state
        for _ in range(count):
            if len(attended) < heads:
                result, *state = attention(
                    order, len(attended), queries, keys, values, rows, columns, parts, state
                )
                attended.append(result)

    def exchange():
        to_send, own = prefixes(order, table, len(owns), arrived, kept, received, levels, half)
        sends.append(to_send)
        owns.append(own)
        others.append(send(to_send, across))

    def fall():
        nonlocal falls, above
        falls += 1
        above = send(
            down(order, table, falls, levels, kept, received, above, dqk // levels, half), downward
        )

    def units_of(memories, base, chunk):
        return [
            (base + unit // 2, unit % 2, attended[base + unit // 2], views_of(memories)[unit])
            for unit in (2 * chunk - 1, 2 * chunk)
            if 0 <= unit < units
        ]

    finished = [0, 0]

    def put(*which):
        nonlocal hidden
        wanted = []
        for i in which:
            wanted += units_of((owns, others)[i], (0, lane_heads)[i], finished[i])
            finished[i] += 1
        hidden = finish(order, wanted, queries, factor, hidden, heads)

    plan = {1: "kaaa", 2: "aa3aa4", 3: "apFd", 4: "wpod", 5: "pwod", 6: "pwo"}
    for step in range(1, steps):
        value, slots = chain_step(order, table, step, kept, received, arrived[-1], levels, half)
        arrived.append((send(value, up), slots))
        for what in plan.get(step, ""):
            if what == "a":
                attend(1)
            elif what == "k":
                kept += views_of(own_memories(order, keys, columns, values, range(2, lane_heads), heads))
            elif what in "234":
                wait(order, taken[int(what)])
            elif what == "f":
                final_normal, tops = finals(order, gathered)
            elif what == "F" and len(attended) == heads:
                factor = factors(order, columns, top_row, *state, heads, dqk)
            elif what == "p" and len(owns) + levels - 2 < step:
                exchange()
            elif what == "d" and falls < levels - 1:
                fall()
            elif what in "wo" and factor is not None and finished["wo".index(what)] < len(owns):
                put("wo".index(what))
            elif what == "b" and min(finished) < len(owns):
                put(0, 1)
    attend(heads)
    if factor is None:
        factor = factors(order, columns, top_row, *state, heads, dqk)
    while len(owns) < chunks:
        exchange()
    while falls < levels - 1:
        fall()
    partner = send(outgoing(order, table, kept, received, above), across)
    if final_normal is None:
        final_normal, tops = finals(order, gathered)
    while finished[0] < chunks:
        put(0)
    while finished[1] < chunks - 1:
        put(1)
    hidden, final_memory = last(
        order, units_of(others, lane_heads, chunks - 1), queries, factor, hidden, heads, table, above, partner,
        kept, received, views_of(owns), views_of(sends), views_of(others),
    )
    return hidden, final_memory, final_normal, tops.reshape(heads)


def solution(mesh):
    token_spec = P(("seq", "ctx"), None)
    gate_spec = P(None, ("seq", "ctx"))
    return jax.shard_map(
        functools.partial(shards, blocks=mesh.shape["ctx"]),
        mesh=mesh,
        in_specs=(token_spec, token_spec, token_spec, gate_spec, gate_spec),
        out_specs=(token_spec, P("seq", "ctx", None), P("seq", "ctx"), P("seq")),
        check_vma=False,
    )
```

```python
import functools

import jax
import jax.numpy as jnp
from jax import lax
from jax.experimental import pallas as pl
from jax.experimental.pallas import tpu as pltpu
from jax.sharding import PartitionSpec as P

VERY_NEGATIVE = -1e30
LANES = 128
MIB = 1 << 20
AXIS = "ctx"

(
    ROW_A, ROW_SEND_P, ROW_SEND_S, ROW_OWN_P, ROW_OWN_S, ROW_FIN_P, ROW_FIN_K, ROW_FIN_R, ROW_CHAIN,
) = range(9)


def chunks_of(heads):
    sizes = (1,1,2,2,2)
    result, head = [], 0
    while head < heads:
        size = min(sizes[min(len(result), len(sizes) - 1)], heads - head)
        result.append(list(range(head, head + size)))
        head += size
    return result


class Order:
    def __init__(self):
        self.last = None
        self.held = []


def call(order, kernel, operands, outs, name, mib=8, scratch=(), aliases=None, flops=0):
    in_specs, arrays = [], []
    count = len(operands)
    for extra in [order.last, *order.held]:
        if extra is not None and not any(extra is operand for operand in operands):
            operands = [*operands, extra]
    body = lambda *refs: kernel(*refs[:count], *refs[len(operands) :])
    for operand in operands:
        if isinstance(operand, tuple):
            in_specs.append(pl.BlockSpec(memory_space=pl.ANY))
            arrays.append(pltpu.with_memory_space_constraint(operand[0], pltpu.HBM))
        else:
            in_specs.append(pl.BlockSpec(memory_space=pltpu.VMEM))
            arrays.append(pltpu.with_memory_space_constraint(operand, pltpu.VMEM))
    out_specs = [
        pl.BlockSpec(memory_space=pl.ANY if out.memory_space == pltpu.HBM else pltpu.VMEM) for out in outs
    ]
    results = pl.pallas_call(
        body,
        in_specs=in_specs,
        out_specs=out_specs,
        out_shape=list(outs),
        scratch_shapes=list(scratch),
        input_output_aliases=aliases or {},
        compiler_params=pltpu.CompilerParams(vmem_limit_bytes=mib * MIB),
        cost_estimate=pl.CostEstimate(flops=int(flops), bytes_accessed=0, transcendentals=0),
        name=name,
    )(*arrays)
    order.last = results[-1]
    return results


class Operands:
    def __init__(self):
        self.arrays = []

    def place(self, array):
        for i, other in enumerate(self.arrays):
            if other is array:
                return i
        self.arrays.append(array)
        return len(self.arrays) - 1

    def view(self, view):
        return self.place(view[0]), view[1]


def position():
    place = lax.axis_index(AXIS)
    return lax.rem(place, 2), lax.div(place, 2)


def lane_iota(shape):
    return lax.broadcasted_iota(jnp.int32, shape, len(shape) - 1)


def row_iota(shape):
    return lax.broadcasted_iota(jnp.int32, shape, 0)


def columns_of(head, width):
    return pl.ds(pl.multiple_of(head * width, width), width)


def three_parts(value):
    high = value.astype(jnp.bfloat16).astype(jnp.float32)
    middle = (value - high).astype(jnp.bfloat16).astype(jnp.float32)
    return high, middle, value - high - middle


def memory_of(key, value, weight):
    scaled = (key.astype(jnp.float32) * weight).astype(jnp.bfloat16)
    return lax.dot_general(
        scaled, value, (((0,), (0,)), ((), ())), preferred_element_type=jnp.float32
    )


def start_kernel(
    input_hbm, forget_hbm, keys_hbm, values_hbm,
    keys_ref, value_ref, rows_ref, columns_ref, summary_ref, input_ref, forget_ref, sems,
):
    heads, tokens = input_ref.shape
    dqk = keys_ref.shape[1] // heads
    dv = value_ref.shape[1]
    copies = [
        pltpu.make_async_copy(forget_hbm, forget_ref, sems.at[0]),
        pltpu.make_async_copy(input_hbm, input_ref, sems.at[1]),
        pltpu.make_async_copy(keys_hbm, keys_ref, sems.at[2]),
        pltpu.make_async_copy(values_hbm.at[:, 0:dv], value_ref, sems.at[3]),
    ]
    for copy in copies:
        copy.start()
    copies[0].wait()
    copies[1].wait()

    gate = forget_ref[...]
    cumulated = jnp.minimum(gate, 0.0) - jnp.log1p(jnp.exp(-jnp.abs(gate)))
    lanes = lane_iota((heads, tokens))
    step = 1
    while step < tokens:
        cumulated = cumulated + jnp.where(lanes >= step, pltpu.roll(cumulated, step, 1), 0.0)
        step *= 2
    level = input_ref[...] - cumulated
    running = level
    step = 1
    while step < tokens:
        running = jnp.maximum(
            running, jnp.where(lanes >= step, pltpu.roll(running, step, 1), VERY_NEGATIVE)
        )
        step *= 2
    highest = running[:, tokens - 1 : tokens]
    decay = cumulated[:, tokens - 1 : tokens]
    weight = jnp.exp(level - highest)
    rows_ref[...] = level
    filler = jnp.zeros((LANES - 3 * heads, tokens), jnp.float32)
    columns_ref[...] = jnp.concatenate([weight, running, cumulated, filler], axis=0).T

    copies[2].wait()
    spare = jnp.zeros((-(-3 * heads // 16) * 16 - 3 * heads, tokens), jnp.float32)
    parts = jnp.concatenate([*three_parts(weight), spare], axis=0).astype(jnp.bfloat16)
    sums = []
    for i in range(heads):
        product = jnp.dot(
            parts, keys_ref[:, i * dqk : (i + 1) * dqk], preferred_element_type=jnp.float32
        )
        sums.append(
            product[i : i + 1] + product[heads + i : heads + i + 1] + product[2 * heads + i : 2 * heads + i + 1]
        )
    lane = lane_iota((heads, LANES))
    stats = jnp.where(lane == 0, decay + highest, jnp.where(lane == 1, decay, 0.0))
    summary_ref[...] = jnp.concatenate([jnp.concatenate(sums, axis=0), stats], axis=1)
    copies[3].wait()


def start(order, input_gate, forget_gate, keys, values):
    heads, tokens = input_gate.shape
    dqk, dv = keys.shape[1] // heads, values.shape[1] // heads
    return call(
        order,
        start_kernel,
        [(a, pl.ANY) for a in (input_gate, forget_gate, keys, values)],
        [
            pltpu.VMEM(keys.shape, keys.dtype),
            pltpu.VMEM((tokens, dv), values.dtype),
            pltpu.VMEM((heads, tokens), jnp.float32),
            pltpu.VMEM((tokens, LANES), jnp.float32),
            pltpu.VMEM((heads, dqk + LANES), jnp.float32),
        ],
        "start",
        mib=12,
        scratch=[
            pltpu.VMEM((heads, tokens), jnp.float32),
            pltpu.VMEM((heads, tokens), jnp.float32),
            pltpu.SemaphoreType.DMA((4,)),
        ],
    )


def load_kernel(in_hbm, out_ref, sem):
    copy = pltpu.make_async_copy(in_hbm, out_ref, sem)
    copy.start()
    copy.wait()


def load(order, array):
    return call(
        order,
        load_kernel,
        [(array, pl.ANY)],
        [pltpu.VMEM(array.shape, array.dtype)],
        "load",
        scratch=[pltpu.SemaphoreType.DMA],
    )[0]


def memories_kernel(keys_ref, columns_ref, values_ref, *refs, heads, first, count, with_summary, with_queries):
    if with_summary:
        summary_ref, away_ref, kept_ref = refs
        rest = away_ref.shape[0] - kept_ref.shape[0], away_ref.shape[1] - summary_ref.shape[1]
        away_ref[kept_ref.shape[0] :, :] = jnp.concatenate(
            [summary_ref[...], jnp.zeros(rest, jnp.float32)], axis=1
        )
    elif with_queries:
        queries_hbm, away_ref, kept_ref, queries_ref, sem = refs
        copy = pltpu.make_async_copy(queries_hbm, queries_ref, sem)
        copy.start()
    else:
        away_ref, kept_ref = refs
    side, _ = position()
    dqk = keys_ref.shape[1] // heads
    rows, dv = kept_ref.shape[0] // count, kept_ref.shape[1]
    stripe = dqk // lax.axis_size(AXIS)
    for i in range(count):
        head = first + i
        value = values_ref[...] if with_summary else values_ref[:, head * dv : (head + 1) * dv]
        memory = memory_of(keys_ref[:, head * dqk : (head + 1) * dqk], value, columns_ref[:, head : head + 1])
        memory = memory.reshape(rows // stripe, 2, stripe, dv)
        low, high = memory[:, 0].reshape(rows, dv), memory[:, 1].reshape(rows, dv)
        here = pl.ds(i * rows, rows)
        away_ref[here, :] = jnp.where(side == 0, high, low)
        kept_ref[here, :] = jnp.where(side == 0, low, high)
    if with_queries:
        copy.wait()


def memories(order, keys, columns, values, chunk, heads, summary=None, queries=None):
    tokens = keys.shape[0]
    dqk = keys.shape[1] // heads
    dv = values.shape[1] // (heads if summary is None else 1)
    more = [] if queries is None else [(queries, pl.ANY)]
    rows = len(chunk) * dqk // 2
    behind = 0 if summary is None else summary.shape[0]
    return call(
        order,
        functools.partial(
            memories_kernel, heads=heads, first=chunk[0], count=len(chunk), with_summary=behind > 0,
            with_queries=bool(more),
        ),
        [keys, columns, values, *([] if summary is None else [summary]), *more],
        [pltpu.VMEM((rows + behind, dv), jnp.float32), pltpu.VMEM((rows, dv), jnp.float32)]
        + [pltpu.VMEM(a.shape, a.dtype) for a, _ in more],
        "memories",
        mib=12,
        scratch=[pltpu.SemaphoreType.DMA] * len(more),
    )


def block_summary(gathered_ref, block, side, level):
    levels = gathered_ref.shape[0]
    turn = lax.rem(block // 2 - level + levels, levels)
    same, other = gathered_ref[turn, 0], gathered_ref[turn, 1]
    return jnp.where(side == block % 2, same, other)


def weights_kernel(gathered_ref, table_ref, parts_ref, top_row_ref):
    levels, _, heads, width = gathered_ref.shape
    blocks = 2 * levels
    dqk = width - LANES
    side, level = position()

    tops, decays, normals = [], [], []
    for block in range(blocks):
        held = block_summary(gathered_ref, block, side, level)
        normals.append(held[:, :dqk])
        tops.append(held[:, dqk : dqk + 1])
        decays.append(held[:, dqk + 1 : dqk + 2])

    pick = lambda at, value, otherwise: jnp.where(level == at, value, otherwise)
    top = jnp.full((heads, 1), VERY_NEGATIVE, jnp.float32)
    normal = jnp.zeros((heads, dqk), jnp.float32)
    zero = jnp.zeros((heads, 1), jnp.float32)
    mine_a = mine_b = mine_first = mine_second = zero
    carry_p = carry_s = zero
    prefix_top, prefix_normal = zero, normal
    scales = []
    for z in range(levels):
        t0, t1, d0, d1 = tops[2 * z], tops[2 * z + 1], decays[2 * z], decays[2 * z + 1]
        pair_top = jnp.maximum(t0 + d1, t1)
        first, second = jnp.exp(t0 + d1 - pair_top), jnp.exp(t1 - pair_top)
        pair_normal = normals[2 * z] * first + normals[2 * z + 1] * second
        middle_top = jnp.maximum(top + d0, t0)
        alpha, beta = jnp.exp(top + d0 - middle_top), jnp.exp(t0 - middle_top)
        middle_normal = normal * alpha + normals[2 * z] * beta
        pair_decay = d0 + d1
        next_top = jnp.maximum(top + pair_decay, pair_top)
        a, b = jnp.exp(top + pair_decay - next_top), jnp.exp(pair_top - next_top)
        mine_a, mine_b = pick(z, a, mine_a), pick(z, b, mine_b)
        mine_first, mine_second = pick(z, first, mine_first), pick(z, second, mine_second)
        carry_p, carry_s = pick(z, alpha, carry_p), pick(z, beta, carry_s)
        prefix_top = pick(z, jnp.where(side == 0, top, middle_top), prefix_top)
        prefix_normal = pick(z, jnp.where(side == 0, normal, middle_normal), prefix_normal)
        normal = normal * a + pair_normal * b
        top = next_top
        scales.append((a, b))
    later = jnp.ones((heads, 1), jnp.float32)
    final_p = final_l = zero
    for z in reversed(range(levels)):
        a, b = scales[z]
        final_l = pick(z, b * later, final_l)
        later = later * a
        final_p = pick(z, later, final_p)

    one = jnp.ones((heads, 1), jnp.float32)
    by_side = lambda zero_value, one_value: jnp.where(side == 0, zero_value, one_value)
    lanes = lane_iota((heads, LANES))
    rows = row_iota((heads, LANES))
    chunks = chunks_of(heads)
    head_of_step = jnp.zeros((heads, LANES), jnp.int32)
    for z in range(levels):
        for c, chunk in enumerate(chunks):
            for slot, head in enumerate(chunk):
                wanted = (lanes == 2 * (c + z) + slot) & (level == z)
                head_of_step = jnp.where(wanted, head, head_of_step)

    def spread(column, heads_wanted):
        return jnp.sum(jnp.where(rows == heads_wanted, column, 0.0), axis=0, keepdims=True)

    mine_own = by_side(mine_first, mine_second)
    mine_partner = by_side(mine_second, mine_first)
    chain_own = spread(mine_b * mine_own, head_of_step)
    chain_partner = spread(mine_b * mine_partner, head_of_step)
    entries = [
        spread(mine_a, head_of_step),
        spread(by_side(carry_p, one), lanes),
        spread(by_side(carry_s, zero), lanes),
        spread(by_side(one, carry_p), lanes),
        spread(by_side(zero, carry_s), lanes),
        spread(final_p, lanes),
        spread(final_l * mine_own, lanes),
        spread(final_l * mine_partner, lanes),
    ]
    for z in range(levels):
        entries += [pick(z, chain_own, 0.0), pick(z, chain_partner, 0.0)]
    here = jnp.ones((1, LANES), jnp.float32)
    entries += [pick(z, here, 0.0) for z in range(levels)]
    empty = jnp.zeros((1, LANES), jnp.float32)
    entries += [empty] * (table_ref.shape[0] - len(entries))
    table_ref[...] = jnp.concatenate(entries, axis=0)

    filler = jnp.zeros((LANES - 3 * heads, dqk), jnp.float32)
    parts = jnp.concatenate([*three_parts(prefix_normal), filler], axis=0)
    parts_ref[...] = parts.T
    prefix_top = jnp.broadcast_to(prefix_top, (heads, LANES))
    filler = jnp.zeros((LANES - heads, LANES), jnp.float32)
    top_row_ref[...] = jnp.concatenate([prefix_top, filler], axis=0).T[:8]


def weights(order, gathered):
    levels, _, heads, width = gathered.shape
    dqk = width - LANES
    table_rows = -(-(ROW_CHAIN + 3 * levels) // 8) * 8
    return call(
        order,
        weights_kernel,
        [gathered],
        [
            pltpu.VMEM((table_rows, LANES), jnp.float32),
            pltpu.VMEM((dqk, LANES), jnp.float32),
            pltpu.VMEM((8, LANES), jnp.float32),
        ],
        "weights",
    )


def wait_kernel(ref, out_ref):
    out_ref[...] = ref[:8, :LANES] if len(ref.shape) == 2 else ref[0, :8, :LANES]


def wait(order, array, flops=0):
    return call(order, wait_kernel, [array], [pltpu.VMEM((8, LANES), jnp.float32)], "wait", flops=flops)[0]


def pair_kernel(summary_ref, taken_ref, out_ref):
    heads, width = summary_ref.shape
    out_ref[0] = summary_ref[...]
    out_ref[1] = taken_ref[taken_ref.shape[0] - heads :, :width]


def pair_of(order, summary, taken):
    return call(order, pair_kernel, [summary, taken], [pltpu.VMEM((2,) + summary.shape, jnp.float32)], "pair")[0]


def pack_kernel(*refs):
    *in_refs, out_ref = refs
    at = 0
    for ref in in_refs:
        value = ref[...].reshape((-1,) + out_ref.shape[1:])
        count = min(value.shape[0], out_ref.shape[0] - at)
        out_ref[at : at + count] = value[:count]
        at += count


def pack(order, arrays, count):
    return call(order, pack_kernel, arrays, [pltpu.VMEM((count,) + arrays[0].shape[1:], jnp.float32)], "pack")[0]


def finals_kernel(gathered_ref, normal_hbm, tops_hbm, token_ref, normal_ref, tops_ref, sems):
    token_ref[...] = jnp.zeros_like(token_ref)
    levels, _, heads, width = gathered_ref.shape
    dqk = width - LANES
    side, level = position()
    top = jnp.full((heads, 1), VERY_NEGATIVE, jnp.float32)
    normal = jnp.zeros((heads, dqk), jnp.float32)
    for block in range(2 * levels):
        held = block_summary(gathered_ref, block, side, level)
        block_top, decay = held[:, dqk : dqk + 1], held[:, dqk + 1 : dqk + 2]
        next_top = jnp.maximum(top + decay, block_top)
        normal = normal * jnp.exp(top + decay - next_top) + held[:, :dqk] * jnp.exp(block_top - next_top)
        top = next_top
    share = normal_hbm.shape[1]
    place = 2 * level + side
    mine = pltpu.roll(normal, lax.rem(dqk - place * share, dqk), 1)
    normal_ref[...] = mine[:, :share]
    filler = jnp.zeros((LANES - heads, LANES), jnp.float32)
    tops = jnp.concatenate([jnp.broadcast_to(top, (heads, LANES)), filler], axis=0).T
    tops_ref[...] = tops[0:1, :heads]
    copies = [
        pltpu.make_async_copy(normal_ref, normal_hbm, sems.at[0]),
        pltpu.make_async_copy(tops_ref, tops_hbm, sems.at[1]),
    ]
    for copy in copies:
        copy.start()
    for copy in copies:
        copy.wait()


def finals(order, gathered):
    levels, _, heads, width = gathered.shape
    shape = (heads, (width - LANES) // (2 * levels))
    normal, tops, _ = call(
        order,
        finals_kernel,
        [gathered],
        [
            pltpu.HBM(shape, jnp.float32),
            pltpu.HBM((1, heads), jnp.float32),
            pltpu.VMEM((8, LANES), jnp.float32),
        ],
        "finals",
        scratch=[
            pltpu.VMEM(shape, jnp.float32),
            pltpu.VMEM((1, heads), jnp.float32),
            pltpu.SemaphoreType.DMA((2,)),
        ],
    )
    return normal, tops


def attention_kernel(
    queries_ref, keys_ref, values_ref, rows_ref, columns_ref, parts_ref, *refs, heads, index
):
    out_ref, sums_ref, products_ref = refs[-3:]
    tokens = queries_ref.shape[0]
    dqk, dv = queries_ref.shape[1] // heads, values_ref.shape[1] // heads
    key_columns, value_columns = pl.ds(index * dqk, dqk), pl.ds(index * dv, dv)
    tile = min(256, tokens)
    level = rows_ref[index : index + 1, :]
    causal = row_iota((tile, tile)) >= lane_iota((tile, tile))
    part_lanes = lane_iota(parts_ref.shape)
    mine = (lax.rem(part_lanes, heads) == index) & (part_lanes < 3 * heads)
    parts = jnp.where(mine, parts_ref[...], 0.0).astype(jnp.bfloat16)

    for begin in range(0, tokens, tile):
        end = begin + tile
        here = pl.ds(begin, tile)
        query = queries_ref[here, key_columns]
        running = columns_ref[here, heads + index : heads + index + 1]
        total = jnp.zeros((tile, 1), jnp.float32)
        result = None
        for low in range(0, end, tile):
            there = pl.ds(low, tile)
            scores = lax.dot_general(
                query, keys_ref[there, key_columns], (((1,), (1,)), ((), ())), preferred_element_type=jnp.float32
            )
            attn = jnp.exp(level[:, low : low + tile] - running) * scores
            if low == begin:
                attn = jnp.where(causal, attn, 0.0)
            total = total + jnp.sum(attn, axis=1, keepdims=True)
            term = jnp.dot(
                attn.astype(jnp.bfloat16), values_ref[there, value_columns], preferred_element_type=jnp.float32
            )
            result = term if result is None else result + term
        product = jnp.dot(query, parts, preferred_element_type=jnp.float32)
        lanes = lane_iota((tile, LANES))
        if len(refs) > 3:
            sums_ref[here, :] = jnp.where(lanes == index, total, refs[0][here, :])
            products_ref[here, :] = refs[1][here, :] + product
        else:
            sums_ref[here, :] = jnp.where(lanes == index, total, 0.0)
            products_ref[here, :] = product
        out_ref[here, :] = result.astype(jnp.bfloat16)


def attention(order, index, queries, keys, values, rows, columns, parts, state):
    tokens = queries.shape[0]
    heads = rows.shape[0]
    dqk, dv = queries.shape[1] // heads, values.shape[1] // heads
    return call(
        order,
        functools.partial(attention_kernel, heads=heads, index=index),
        [queries, keys, values, rows, columns, parts, *state],
        [
            pltpu.VMEM((tokens, dv), jnp.bfloat16),
            pltpu.VMEM((tokens, LANES), jnp.float32),
            pltpu.VMEM((tokens, LANES), jnp.float32),
        ],
        "attention",
        mib=12,
    )


def factors_kernel(columns_ref, top_ref, sums_ref, products_ref, out_ref, *, heads, dqk):
    tokens = columns_ref.shape[0]
    tile = min(256, tokens)
    shift = lambda block, by: pltpu.roll(block, (LANES - by) % LANES, 1)
    for begin in range(0, tokens, tile):
        here = pl.ds(begin, tile)
        product = products_ref[here, :]
        product = product + shift(product, heads) + shift(product, 2 * heads)
        column = columns_ref[here, :]
        running, cumulated = shift(column, heads), shift(column, 2 * heads)
        top = top_ref[0:1, :]
        highest = jnp.maximum(running, top)
        scaling = float(dqk) ** -0.5
        local, carried = jnp.exp(running - highest), jnp.exp(top - highest)
        denominator = (local * sums_ref[here, :] + carried * product) * scaling
        divisor = jnp.maximum(jnp.abs(denominator), jnp.exp(-(cumulated + highest)))
        inverse = scaling / divisor
        out_ref[here, :] = jnp.where(
            lane_iota((tile, LANES)) < heads, local * inverse, pltpu.roll(carried * inverse, heads, 1)
        )


def factors(order, columns, top_row, sums, products, heads, dqk):
    return call(
        order,
        functools.partial(factors_kernel, heads=heads, dqk=dqk),
        [columns, top_row, sums, products],
        [pltpu.VMEM(columns.shape, jnp.float32)],
        "factors",
    )[0]


def finish_heads(queries_ref, factors_ref, refs, items, heads, out_hbm, memory, scratch, sems):
    side, _ = position()
    tokens = queries_ref.shape[0]
    dqk = queries_ref.shape[1] // heads
    dv = scratch.shape[2]
    rows = dqk // 2
    stripe = dqk // lax.axis_size(AXIS)
    tile = min(256, tokens)
    copies = []
    for at, (head, held, own, other) in enumerate(items):
        own = refs[own[0]][own[1] : own[1] + rows, :].astype(jnp.bfloat16)
        other = refs[other[0]][other[1] : other[1] + rows, :].astype(jnp.bfloat16)
        low, high = jnp.where(side == 0, own, other), jnp.where(side == 0, other, own)
        for i in range(rows // stripe):
            memory[2 * i * stripe : (2 * i + 1) * stripe, :] = low[i * stripe : (i + 1) * stripe]
            memory[(2 * i + 1) * stripe : (2 * i + 2) * stripe, :] = high[i * stripe : (i + 1) * stripe]
        prefix = memory[...]
        for begin in range(0, tokens, tile):
            here = pl.ds(begin, tile)
            local = factors_ref[here, head : head + 1]
            carried = factors_ref[here, heads + head : heads + head + 1]
            term = jnp.dot(
                queries_ref[here, head * dqk : (head + 1) * dqk], prefix, preferred_element_type=jnp.float32
            )
            value = refs[held][here, :].astype(jnp.float32)
            scratch[at, here, :] = (value * local + term * carried).astype(scratch.dtype)
            copy = pltpu.make_async_copy(
                scratch.at[at, here, :], out_hbm.at[here, pl.ds(head * dv, dv)], sems.at[len(copies)]
            )
            copy.start()
            copies.append(copy)
    return copies


def finish_kernel(queries_ref, factors_ref, *refs, items, heads):
    *_, out_hbm, token_ref, memory, scratch, sems = refs
    token_ref[...] = jnp.zeros_like(token_ref)
    for copy in finish_heads(queries_ref, factors_ref, refs, items, heads, out_hbm, memory, scratch, sems):
        copy.wait()


def finish_operands(wanted):
    operands = Operands()
    items = [
        (head, operands.place(held), operands.view(own), operands.view(other)) for head, held, own, other in wanted
    ]
    return operands, items


def finish_scratch(wanted, tokens):
    dv = wanted[0][1].shape[1]
    rows = wanted[0][2][0].shape[0] // wanted[0][2][2]
    return [
        pltpu.VMEM((2 * rows, dv), jnp.bfloat16),
        pltpu.VMEM((len(wanted), tokens, dv), jnp.bfloat16),
        pltpu.SemaphoreType.DMA((len(wanted) * max(1, tokens // 256),)),
    ]


def finish(order, wanted, queries, factor, hidden, heads):
    operands, items = finish_operands(wanted)
    tokens = queries.shape[0]
    dv = wanted[0][1].shape[1]
    arrays = [queries, factor, *operands.arrays]
    aliases = {}
    if hidden is not None:
        aliases = {len(arrays): 0}
        arrays.append((hidden, pl.ANY))
    return call(
        order,
        functools.partial(finish_kernel, items=items, heads=heads),
        arrays,
        [pltpu.HBM((tokens, heads * dv), jnp.bfloat16), pltpu.VMEM((8, LANES), jnp.float32)],
        "finish",
        mib=12,
        scratch=finish_scratch(wanted, tokens),
        aliases=aliases,
    )[0]


def entry_of(table_ref):
    return lambda row, lane: table_ref[row : row + 1, lane : lane + 1]


def row_tiles(rows):
    tile = min(16, rows)
    return [(begin, tile) for begin in range(0, rows, tile)]


def chain_kernel(table_ref, *refs, slots):
    out_ref = refs[-1]
    entry = entry_of(table_ref)
    rows = out_ref.shape[0] // len(slots)
    for i, terms in enumerate(slots):
        terms = [(place, row, entry(which, lane)) for (place, row), which, lane in terms]
        for begin, size in row_tiles(rows):
            total = None
            for place, row, weight in terms:
                term = refs[place][row + begin : row + begin + size, :] * weight
                total = term if total is None else total + term
            out_ref[i * rows + begin : i * rows + begin + size, :] = total


def first_kernel(pair_ref, keep_ref, take_ref, out_ref):
    side, _ = position()
    width = pair_ref.shape[2]
    top, decay = [], []
    for which in range(2):
        top.append(pair_ref[which, 0:1, width - LANES : width - LANES + 1])
        decay.append(pair_ref[which, 0:1, width - LANES + 1 : width - LANES + 2])
    own = top[0] + jnp.where(side == 0, decay[1], 0.0)
    partner = top[1] + jnp.where(side == 0, 0.0, decay[0])
    highest = jnp.maximum(own, partner)
    own, partner = jnp.exp(own - highest), jnp.exp(partner - highest)
    for begin, size in row_tiles(out_ref.shape[0]):
        here = pl.ds(begin, size)
        out_ref[here, :] = keep_ref[here, :] * own + take_ref[here, :] * partner


def first_step(order, pair, keep, take):
    return call(
        order, first_kernel, [pair, keep, take], [pltpu.VMEM(keep.shape, jnp.float32)], "chain"
    )[0]


def chain_step(order, table, step, chunks, kept, received, earlier, levels):
    operands = Operands()
    slots = []
    for slot in range(2):
        terms = []
        lane = 2 * step + slot
        for z in range(levels - 1):
            if 0 <= step - z < len(chunks) and slot < len(chunks[step - z]):
                head = chunks[step - z][slot]
                terms.append((operands.view(kept[head]), ROW_CHAIN + 2 * z, lane))
                terms.append((operands.view(received[head]), ROW_CHAIN + 2 * z + 1, lane))
        if terms:
            if slot < earlier[2]:
                terms.append((operands.view((earlier[0], slot * earlier[1], earlier[2])), ROW_A, lane))
            slots.append(terms)
    rows, dv = earlier[1], earlier[0].shape[1]
    value = call(
        order,
        functools.partial(chain_kernel, slots=slots),
        [table, *operands.arrays],
        [pltpu.VMEM((rows * len(slots), dv), jnp.float32)],
        "chain",
    )[0]
    return value, rows, len(slots)


def prefix_kernel(table_ref, *refs, levels, pieces):
    send_ref, own_ref = refs[-2:]
    rows = send_ref.shape[0] // len(pieces)
    entry = entry_of(table_ref)
    here_row = ROW_CHAIN + 2 * levels
    picks = [entry(here_row + z, 0) for z in range(1, levels)]
    for i, (head, arrivals, (keep, keep_row), (take, take_row)) in enumerate(pieces):
        send_p, send_s = entry(ROW_SEND_P, head), entry(ROW_SEND_S, head)
        own_p, own_s = entry(ROW_OWN_P, head), entry(ROW_OWN_S, head)
        for begin, size in row_tiles(rows):
            prefix = None
            for (place, row), weight in zip(arrivals, picks):
                term = refs[place][row + begin : row + begin + size, :] * weight
                prefix = term if prefix is None else prefix + term
            here = pl.ds(i * rows + begin, size)
            send_ref[here, :] = prefix * send_p + refs[keep][keep_row + begin : keep_row + begin + size, :] * send_s
            own_ref[here, :] = prefix * own_p + refs[take][take_row + begin : take_row + begin + size, :] * own_s


def prefixes(order, table, index, chunks, arrived, kept, received, levels):
    operands = Operands()
    pieces = []
    for slot, head in enumerate(chunks[index]):
        arrivals = []
        for z in range(1, levels):
            array, rows, count = arrived[index + z - 1]
            arrivals.append(operands.view((array, slot * rows, count)))
        pieces.append((head, arrivals, operands.view(kept[head]), operands.view(received[head])))
    out = pltpu.VMEM((len(pieces) * arrived[0][1], kept[0][0].shape[1]), jnp.float32)
    return call(
        order,
        functools.partial(prefix_kernel, levels=levels, pieces=pieces),
        [table, *operands.arrays],
        [out, out],
        "prefix",
    )


def level_rows(table_ref, refs, views, level, stripe):
    entry = entry_of(table_ref)
    for head, ((keep, keep_row), (take, take_row)) in enumerate(views):
        here = lambda row: pl.ds(pl.multiple_of(row + level * stripe, stripe), stripe)
        yield (
            head,
            refs[keep][here(keep_row), :] * entry(ROW_FIN_K, head)
            + refs[take][here(take_row), :] * entry(ROW_FIN_R, head),
        )


def down_kernel(table_ref, *refs, step, levels, views, earlier):
    out_ref = refs[-1]
    stripe = out_ref.shape[1]
    _, level = position()
    target = jnp.maximum(step - levels + level, 0)
    for head, value in level_rows(table_ref, refs, views, target, stripe):
        out_ref[head] = value if earlier is None else value + refs[earlier][head]


def down(order, table, step, levels, kept, received, earlier, stripe):
    operands = Operands()
    views = [(operands.view(keep), operands.view(take)) for keep, take in zip(kept, received)]
    place = None if earlier is None else operands.place(earlier)
    return call(
        order,
        functools.partial(down_kernel, step=step, levels=levels, views=views, earlier=place),
        [table, *operands.arrays],
        [pltpu.VMEM((len(kept), stripe, kept[0][0].shape[1]), jnp.float32)],
        "down",
    )[0]


def last_kernel(queries_ref, factors_ref, table_ref, above_ref, *refs, items, heads, views, prefix_views):
    out_hbm, final_hbm, token_ref, memory, scratch, sems, final_ref, final_sem = refs[-8:]
    token_ref[...] = jnp.zeros_like(token_ref)
    copies = finish_heads(queries_ref, factors_ref, refs, items, heads, out_hbm, memory, scratch, sems)
    side, level = position()
    stripe = above_ref.shape[1]
    entry = entry_of(table_ref)
    for head, value in level_rows(table_ref, refs, views, level, stripe):
        (own, own_row), (sent, sent_row) = prefix_views[head]
        here = lambda row: pl.ds(pl.multiple_of(row + level * stripe, stripe), stripe)
        prefix = jnp.where(side == 0, refs[own][here(own_row), :], refs[sent][here(sent_row), :])
        final_ref[head] = value + prefix * entry(ROW_FIN_P, head) + above_ref[head]
    copies.append(pltpu.make_async_copy(final_ref, final_hbm, final_sem))
    copies[-1].start()
    for copy in copies:
        copy.wait()


def last(order, wanted, queries, factor, hidden, heads, table, above, kept, received, owns, sends):
    operands, items = finish_operands(wanted)
    views = [(operands.view(keep), operands.view(take)) for keep, take in zip(kept, received)]
    prefix_views = [(operands.view(own), operands.view(sent)) for own, sent in zip(owns, sends)]
    tokens = queries.shape[0]
    dv = wanted[0][1].shape[1]
    arrays = [queries, factor, table, above, *operands.arrays, (hidden, pl.ANY)]
    return call(
        order,
        functools.partial(last_kernel, items=items, heads=heads, views=views, prefix_views=prefix_views),
        arrays,
        [
            pltpu.HBM((tokens, heads * dv), jnp.bfloat16),
            pltpu.HBM(above.shape, jnp.float32),
            pltpu.VMEM((8, LANES), jnp.float32),
        ],
        "last",
        mib=12,
        scratch=[
            *finish_scratch(wanted, tokens),
            pltpu.VMEM(above.shape, jnp.float32),
            pltpu.SemaphoreType.DMA,
        ],
        aliases={len(arrays) - 1: 0},
    )[:2]


def shards(queries, keys, values, input_gate, forget_gate, *, blocks):
    heads = input_gate.shape[0]
    dqk, dv = queries.shape[1] // heads, values.shape[1] // heads
    rows_of_unit = dqk // 2
    levels = blocks // 2
    across = [(i, i ^ 1) for i in range(blocks)]
    up = [(i, i + 2) for i in range(blocks - 2)]
    downward = [(i + 2, i) for i in range(blocks - 2)]
    send = lambda value, pairs: lax.ppermute(value, AXIS, pairs)
    order = Order()
    chunks = chunks_of(heads)
    steps = len(chunks) + levels - 2

    def views_of(arrays):
        return [
            (array, slot * rows_of_unit, len(chunk))
            for array, chunk in zip(arrays, chunks)
            for slot in range(len(chunk))
        ]

    keys, first_value, rows, columns, summary = start(order, input_gate, forget_gate, keys, values)
    taken, kept = [], []

    def remember(held_values, chunk, **more):
        away, keep, *rest = memories(order, keys, columns, held_values, chunk, heads, **more)
        taken.append(send(away, across))
        kept.append(keep)
        return rest

    remember(first_value, chunks[0], summary=summary)
    values = load(order, values)
    remember(values, chunks[1])

    pair = pair_of(order, summary, taken[0])
    arrived = [(send(first_step(order, pair, kept[0], taken[0]), up), rows_of_unit, 1)]
    gathered = pair[None]
    while gathered.shape[0] < levels:
        reach = gathered.shape[0]
        more = send(gathered, [(i, (i - 2 * reach) % blocks) for i in range(blocks)])
        if reach > 1 and len(taken) < len(chunks) - 1:
            remember(values, chunks[len(taken)])
        gathered = pack(order, [gathered, more], min(2 * reach, levels))
    while len(taken) < len(chunks) - 1:
        remember(values, chunks[len(taken)])
    table, parts, top_row = weights(order, gathered)

    attended, state = [], ()
    sends, owns, others = [], [], []
    hidden = factor = above = final_normal = tops = None
    falls = finished = 0

    def attend(count):
        nonlocal state
        for _ in range(count):
            if len(attended) < heads:
                result, *state = attention(
                    order, len(attended), queries, keys, values, rows, columns, parts, state
                )
                attended.append(result)

    def exchange():
        to_send, own = prefixes(
            order, table, len(owns), chunks, arrived, views_of(kept), views_of(taken), levels
        )
        sends.append(to_send)
        owns.append(own)
        others.append(send(to_send, across))

    def fall():
        nonlocal falls, above
        falls += 1
        above = send(
            down(order, table, falls, levels, views_of(kept), views_of(taken), above, dqk // blocks), downward
        )

    def wanted(chunk):
        return [(head, attended[head], views_of(owns)[head], views_of(others)[head]) for head in chunks[chunk]]

    def put():
        nonlocal hidden, finished
        hidden = finish(order, wanted(finished), queries, factor, hidden, heads)
        finished += 1

    plan = {1: "ma", 2: "aaaa", 3: "paadx", 4: "paFodx", 5: "pod", 6: "fXpoY"}
    for step in range(1, steps):
        value, unit_rows, count = chain_step(
            order, table, step, chunks, views_of(kept), views_of(taken), arrived[-1], levels
        )
        arrived.append((send(value, up), unit_rows, count))
        for what in plan.get(step, ""):
            if what == "m":
                (queries,) = remember(values, chunks[-1], queries=queries)
            elif what == "a":
                attend(1)
            elif what == "f":
                final_normal, tops = finals(order, gathered)
            elif what == "F" and len(attended) == heads:
                factor = factors(order, columns, top_row, *state, heads, dqk)
            elif what == "p" and len(owns) + levels - 2 < step:
                exchange()
            elif what == "d" and falls < levels - 1:
                fall()
            elif what == "o" and factor is not None and finished < len(owns):
                put()
            elif what == "x" and others:
                wait(order, others[-1])
            elif what == "X" and others:
                wait(order, others[-1], 3e9)
            elif what == "Y" and above is not None:
                wait(order, above, 3e9)
    attend(heads)
    if factor is None:
        factor = factors(order, columns, top_row, *state, heads, dqk)
    while len(owns) < len(chunks):
        exchange()
    while falls < levels - 1:
        fall()
    if final_normal is None:
        final_normal, tops = finals(order, gathered)
    while finished < len(chunks) - 1:
        put()
    hidden, final_memory = last(
        order, wanted(len(chunks) - 1), queries, factor, hidden, heads, table, above,
        views_of(kept), views_of(taken), views_of(owns), views_of(sends),
    )
    return hidden, final_memory, final_normal, tops.reshape(heads)


def solution(mesh):
    token_spec = P(("seq", "ctx"), None)
    gate_spec = P(None, ("seq", "ctx"))
    return jax.shard_map(
        functools.partial(shards, blocks=mesh.shape["ctx"]),
        mesh=mesh,
        in_specs=(token_spec, token_spec, token_spec, gate_spec, gate_spec),
        out_specs=(token_spec, P("seq", "ctx", None), P("seq", "ctx"), P("seq")),
        check_vma=False,
    )
```

```python
import functools

import jax
import jax.numpy as jnp
from jax import lax
from jax.experimental import pallas as pl
from jax.experimental.pallas import tpu as pltpu
from jax.sharding import PartitionSpec as P

VERY_NEGATIVE = -1e30
LANES = 128
MIB = 1 << 20
AXIS = "ctx"

(
    ROW_A, ROW_SEND_P, ROW_SEND_S, ROW_OWN_P, ROW_OWN_S, ROW_FIN_P, ROW_FIN_K, ROW_FIN_R, ROW_CHAIN,
) = range(9)


def chunks_of(heads):
    sizes = (1,1,2,2,2)
    result, head = [], 0
    while head < heads:
        size = min(sizes[min(len(result), len(sizes) - 1)], heads - head)
        result.append(list(range(head, head + size)))
        head += size
    return result


class Order:
    def __init__(self):
        self.last = None
        self.held = []


def call(order, kernel, operands, outs, name, mib=8, scratch=(), aliases=None, flops=0):
    in_specs, arrays = [], []
    count = len(operands)
    for extra in [order.last, *order.held]:
        if extra is not None and not any(extra is operand for operand in operands):
            operands = [*operands, extra]
    body = lambda *refs: kernel(*refs[:count], *refs[len(operands) :])
    for operand in operands:
        if isinstance(operand, tuple):
            in_specs.append(pl.BlockSpec(memory_space=pl.ANY))
            arrays.append(pltpu.with_memory_space_constraint(operand[0], pltpu.HBM))
        else:
            in_specs.append(pl.BlockSpec(memory_space=pltpu.VMEM))
            arrays.append(pltpu.with_memory_space_constraint(operand, pltpu.VMEM))
    out_specs = [
        pl.BlockSpec(memory_space=pl.ANY if out.memory_space == pltpu.HBM else pltpu.VMEM) for out in outs
    ]
    results = pl.pallas_call(
        body,
        in_specs=in_specs,
        out_specs=out_specs,
        out_shape=list(outs),
        scratch_shapes=list(scratch),
        input_output_aliases=aliases or {},
        compiler_params=pltpu.CompilerParams(vmem_limit_bytes=mib * MIB),
        cost_estimate=pl.CostEstimate(flops=int(flops), bytes_accessed=0, transcendentals=0),
        name=name,
    )(*arrays)
    order.last = results[-1]
    return results


class Operands:
    def __init__(self):
        self.arrays = []

    def place(self, array):
        for i, other in enumerate(self.arrays):
            if other is array:
                return i
        self.arrays.append(array)
        return len(self.arrays) - 1

    def view(self, view):
        return self.place(view[0]), view[1]


def position():
    place = lax.axis_index(AXIS)
    return lax.rem(place, 2), lax.div(place, 2)


def lane_iota(shape):
    return lax.broadcasted_iota(jnp.int32, shape, len(shape) - 1)


def row_iota(shape):
    return lax.broadcasted_iota(jnp.int32, shape, 0)


def columns_of(head, width):
    return pl.ds(pl.multiple_of(head * width, width), width)


def three_parts(value):
    high = value.astype(jnp.bfloat16).astype(jnp.float32)
    middle = (value - high).astype(jnp.bfloat16).astype(jnp.float32)
    return high, middle, value - high - middle


def memory_of(key, value, weight):
    scaled = (key.astype(jnp.float32) * weight).astype(jnp.bfloat16)
    return lax.dot_general(
        scaled, value, (((0,), (0,)), ((), ())), preferred_element_type=jnp.float32
    )


def start_kernel(
    input_hbm, forget_hbm, keys_hbm, values_hbm,
    keys_ref, value_ref, rows_ref, columns_ref, summary_ref, input_ref, forget_ref, sems,
):
    heads, tokens = input_ref.shape
    dqk = keys_ref.shape[1] // heads
    dv = values_hbm.shape[1] // heads
    copies = [
        pltpu.make_async_copy(forget_hbm, forget_ref, sems.at[0]),
        pltpu.make_async_copy(input_hbm, input_ref, sems.at[1]),
        pltpu.make_async_copy(keys_hbm, keys_ref, sems.at[2]),
        pltpu.make_async_copy(values_hbm.at[:, 0 : value_ref.shape[1]], value_ref, sems.at[3]),
    ]
    for copy in copies:
        copy.start()
    copies[0].wait()
    copies[1].wait()

    gate = forget_ref[...]
    cumulated = jnp.minimum(gate, 0.0) - jnp.log1p(jnp.exp(-jnp.abs(gate)))
    lanes = lane_iota((heads, tokens))
    step = 1
    while step < tokens:
        cumulated = cumulated + jnp.where(lanes >= step, pltpu.roll(cumulated, step, 1), 0.0)
        step *= 2
    level = input_ref[...] - cumulated
    running = level
    step = 1
    while step < tokens:
        running = jnp.maximum(
            running, jnp.where(lanes >= step, pltpu.roll(running, step, 1), VERY_NEGATIVE)
        )
        step *= 2
    highest = running[:, tokens - 1 : tokens]
    decay = cumulated[:, tokens - 1 : tokens]
    weight = jnp.exp(level - highest)
    rows_ref[...] = level
    filler = jnp.zeros((LANES - 3 * heads, tokens), jnp.float32)
    columns_ref[...] = jnp.concatenate([weight, running, cumulated, filler], axis=0).T

    copies[2].wait()
    spare = jnp.zeros((-(-3 * heads // 16) * 16 - 3 * heads, tokens), jnp.float32)
    parts = jnp.concatenate([*three_parts(weight), spare], axis=0).astype(jnp.bfloat16)
    sums = []
    for i in range(heads):
        product = jnp.dot(
            parts, keys_ref[:, i * dqk : (i + 1) * dqk], preferred_element_type=jnp.float32
        )
        sums.append(
            product[i : i + 1] + product[heads + i : heads + i + 1] + product[2 * heads + i : 2 * heads + i + 1]
        )
    lane = lane_iota((heads, LANES))
    stats = jnp.where(lane == 0, decay + highest, jnp.where(lane == 1, decay, 0.0))
    summary_ref[...] = jnp.concatenate([jnp.concatenate(sums, axis=0), stats], axis=1)
    copies[3].wait()


def start(order, input_gate, forget_gate, keys, values):
    heads, tokens = input_gate.shape
    dqk, dv = keys.shape[1] // heads, values.shape[1] // heads
    return call(
        order,
        start_kernel,
        [(a, pl.ANY) for a in (input_gate, forget_gate, keys, values)],
        [
            pltpu.VMEM(keys.shape, keys.dtype),
            pltpu.VMEM((tokens, len(chunks_of(heads)[0]) * dv), values.dtype),
            pltpu.VMEM((heads, tokens), jnp.float32),
            pltpu.VMEM((tokens, LANES), jnp.float32),
            pltpu.VMEM((heads, dqk + LANES), jnp.float32),
        ],
        "start",
        mib=12,
        scratch=[
            pltpu.VMEM((heads, tokens), jnp.float32),
            pltpu.VMEM((heads, tokens), jnp.float32),
            pltpu.SemaphoreType.DMA((4,)),
        ],
    )


def load_kernel(*refs):
    *refs, sems = refs
    count = len(refs) // 2
    copies = [pltpu.make_async_copy(refs[i], refs[count + i], sems.at[i]) for i in range(count)]
    for copy in copies:
        copy.start()
    for copy in copies:
        copy.wait()


def load(order, arrays):
    return call(
        order,
        load_kernel,
        [(array, pl.ANY) for array in arrays],
        [pltpu.VMEM(array.shape, array.dtype) for array in arrays],
        "load",
        scratch=[pltpu.SemaphoreType.DMA((len(arrays),))],
    )


def memories_kernel(keys_ref, columns_ref, values_ref, *refs, heads, first, count, with_summary):
    *summary_ref, away_ref, kept_ref = refs
    if with_summary:
        rest = away_ref.shape[0] - kept_ref.shape[0], away_ref.shape[1] - summary_ref[0].shape[1]
        away_ref[kept_ref.shape[0] :, :] = jnp.concatenate(
            [summary_ref[0][...], jnp.zeros(rest, jnp.float32)], axis=1
        )
    side, _ = position()
    dqk = keys_ref.shape[1] // heads
    rows, dv = kept_ref.shape[0] // count, kept_ref.shape[1]
    stripe = dqk // lax.axis_size(AXIS)
    for i in range(count):
        head = first + i
        place = i if with_summary else head
        value = values_ref[:, place * dv : (place + 1) * dv]
        memory = memory_of(keys_ref[:, head * dqk : (head + 1) * dqk], value, columns_ref[:, head : head + 1])
        memory = memory.reshape(rows // stripe, 2, stripe, dv)
        low, high = memory[:, 0].reshape(rows, dv), memory[:, 1].reshape(rows, dv)
        here = pl.ds(i * rows, rows)
        away_ref[here, :] = jnp.where(side == 0, high, low)
        kept_ref[here, :] = jnp.where(side == 0, low, high)


def memories(order, keys, columns, values, chunk, heads, summary=None):
    dqk = keys.shape[1] // heads
    dv = values.shape[1] // (heads if summary is None else len(chunk))
    more = [] if summary is None else [summary]
    rows = len(chunk) * dqk // 2
    behind = sum(a.shape[0] for a in more)
    return call(
        order,
        functools.partial(
            memories_kernel, heads=heads, first=chunk[0], count=len(chunk), with_summary=bool(more)
        ),
        [keys, columns, values, *more],
        [pltpu.VMEM((rows + behind, dv), jnp.float32), pltpu.VMEM((rows, dv), jnp.float32)],
        "memories",
        mib=12,
    )


def block_summary(gathered_ref, block, side, level):
    levels = gathered_ref.shape[0]
    turn = lax.rem(block // 2 - level + levels, levels)
    same, other = gathered_ref[turn, 0], gathered_ref[turn, 1]
    return jnp.where(side == block % 2, same, other)


def weights_kernel(gathered_ref, table_ref, parts_ref, top_row_ref):
    levels, _, heads, width = gathered_ref.shape
    blocks = 2 * levels
    dqk = width - LANES
    side, level = position()

    tops, decays, normals = [], [], []
    for block in range(blocks):
        held = block_summary(gathered_ref, block, side, level)
        normals.append(held[:, :dqk])
        tops.append(held[:, dqk : dqk + 1])
        decays.append(held[:, dqk + 1 : dqk + 2])

    pick = lambda at, value, otherwise: jnp.where(level == at, value, otherwise)
    top = jnp.full((heads, 1), VERY_NEGATIVE, jnp.float32)
    normal = jnp.zeros((heads, dqk), jnp.float32)
    zero = jnp.zeros((heads, 1), jnp.float32)
    mine_a = mine_b = mine_first = mine_second = zero
    carry_p = carry_s = zero
    prefix_top, prefix_normal = zero, normal
    scales = []
    for z in range(levels):
        t0, t1, d0, d1 = tops[2 * z], tops[2 * z + 1], decays[2 * z], decays[2 * z + 1]
        pair_top = jnp.maximum(t0 + d1, t1)
        first, second = jnp.exp(t0 + d1 - pair_top), jnp.exp(t1 - pair_top)
        pair_normal = normals[2 * z] * first + normals[2 * z + 1] * second
        middle_top = jnp.maximum(top + d0, t0)
        alpha, beta = jnp.exp(top + d0 - middle_top), jnp.exp(t0 - middle_top)
        middle_normal = normal * alpha + normals[2 * z] * beta
        pair_decay = d0 + d1
        next_top = jnp.maximum(top + pair_decay, pair_top)
        a, b = jnp.exp(top + pair_decay - next_top), jnp.exp(pair_top - next_top)
        mine_a, mine_b = pick(z, a, mine_a), pick(z, b, mine_b)
        mine_first, mine_second = pick(z, first, mine_first), pick(z, second, mine_second)
        carry_p, carry_s = pick(z, alpha, carry_p), pick(z, beta, carry_s)
        prefix_top = pick(z, jnp.where(side == 0, top, middle_top), prefix_top)
        prefix_normal = pick(z, jnp.where(side == 0, normal, middle_normal), prefix_normal)
        normal = normal * a + pair_normal * b
        top = next_top
        scales.append((a, b))
    later = jnp.ones((heads, 1), jnp.float32)
    final_p = final_l = zero
    for z in reversed(range(levels)):
        a, b = scales[z]
        final_l = pick(z, b * later, final_l)
        later = later * a
        final_p = pick(z, later, final_p)

    one = jnp.ones((heads, 1), jnp.float32)
    by_side = lambda zero_value, one_value: jnp.where(side == 0, zero_value, one_value)
    lanes = lane_iota((heads, LANES))
    rows = row_iota((heads, LANES))
    chunks = chunks_of(heads)
    head_of_step = jnp.zeros((heads, LANES), jnp.int32)
    for z in range(levels):
        for c, chunk in enumerate(chunks):
            for slot, head in enumerate(chunk):
                wanted = (lanes == 2 * (c + z) + slot) & (level == z)
                head_of_step = jnp.where(wanted, head, head_of_step)

    def spread(column, heads_wanted):
        return jnp.sum(jnp.where(rows == heads_wanted, column, 0.0), axis=0, keepdims=True)

    mine_own = by_side(mine_first, mine_second)
    mine_partner = by_side(mine_second, mine_first)
    chain_own = spread(mine_b * mine_own, head_of_step)
    chain_partner = spread(mine_b * mine_partner, head_of_step)
    entries = [
        spread(mine_a, head_of_step),
        spread(by_side(carry_p, one), lanes),
        spread(by_side(carry_s, zero), lanes),
        spread(by_side(one, carry_p), lanes),
        spread(by_side(zero, carry_s), lanes),
        spread(final_p, lanes),
        spread(final_l * mine_own, lanes),
        spread(final_l * mine_partner, lanes),
    ]
    for z in range(levels):
        entries += [pick(z, chain_own, 0.0), pick(z, chain_partner, 0.0)]
    here = jnp.ones((1, LANES), jnp.float32)
    entries += [pick(z, here, 0.0) for z in range(levels)]
    empty = jnp.zeros((1, LANES), jnp.float32)
    entries += [empty] * (table_ref.shape[0] - len(entries))
    table_ref[...] = jnp.concatenate(entries, axis=0)

    filler = jnp.zeros((LANES - 3 * heads, dqk), jnp.float32)
    parts = jnp.concatenate([*three_parts(prefix_normal), filler], axis=0)
    parts_ref[...] = parts.T
    prefix_top = jnp.broadcast_to(prefix_top, (heads, LANES))
    filler = jnp.zeros((LANES - heads, LANES), jnp.float32)
    top_row_ref[...] = jnp.concatenate([prefix_top, filler], axis=0).T[:8]


def weights(order, gathered):
    levels, _, heads, width = gathered.shape
    dqk = width - LANES
    table_rows = -(-(ROW_CHAIN + 3 * levels) // 8) * 8
    return call(
        order,
        weights_kernel,
        [gathered],
        [
            pltpu.VMEM((table_rows, LANES), jnp.float32),
            pltpu.VMEM((dqk, LANES), jnp.float32),
            pltpu.VMEM((8, LANES), jnp.float32),
        ],
        "weights",
    )


def wait_kernel(ref, out_ref):
    out_ref[...] = ref[:8, :LANES] if len(ref.shape) == 2 else ref[0, :8, :LANES]


def wait(order, array, flops=0):
    return call(order, wait_kernel, [array], [pltpu.VMEM((8, LANES), jnp.float32)], "wait", flops=flops)[0]


def pair_kernel(summary_ref, taken_ref, out_ref):
    heads, width = summary_ref.shape
    out_ref[0] = summary_ref[...]
    out_ref[1] = taken_ref[taken_ref.shape[0] - heads :, :width]


def pair_of(order, summary, taken):
    return call(order, pair_kernel, [summary, taken], [pltpu.VMEM((2,) + summary.shape, jnp.float32)], "pair")[0]


def pack_kernel(*refs):
    *in_refs, out_ref = refs
    at = 0
    for ref in in_refs:
        value = ref[...].reshape((-1,) + out_ref.shape[1:])
        count = min(value.shape[0], out_ref.shape[0] - at)
        out_ref[at : at + count] = value[:count]
        at += count


def pack(order, arrays, count):
    return call(order, pack_kernel, arrays, [pltpu.VMEM((count,) + arrays[0].shape[1:], jnp.float32)], "pack")[0]


def finals_kernel(gathered_ref, normal_hbm, tops_hbm, token_ref, normal_ref, tops_ref, sems):
    token_ref[...] = jnp.zeros_like(token_ref)
    levels, _, heads, width = gathered_ref.shape
    dqk = width - LANES
    side, level = position()
    top = jnp.full((heads, 1), VERY_NEGATIVE, jnp.float32)
    normal = jnp.zeros((heads, dqk), jnp.float32)
    for block in range(2 * levels):
        held = block_summary(gathered_ref, block, side, level)
        block_top, decay = held[:, dqk : dqk + 1], held[:, dqk + 1 : dqk + 2]
        next_top = jnp.maximum(top + decay, block_top)
        normal = normal * jnp.exp(top + decay - next_top) + held[:, :dqk] * jnp.exp(block_top - next_top)
        top = next_top
    share = normal_hbm.shape[1]
    place = 2 * level + side
    mine = pltpu.roll(normal, lax.rem(dqk - place * share, dqk), 1)
    normal_ref[...] = mine[:, :share]
    filler = jnp.zeros((LANES - heads, LANES), jnp.float32)
    tops = jnp.concatenate([jnp.broadcast_to(top, (heads, LANES)), filler], axis=0).T
    tops_ref[...] = tops[0:1, :heads]
    copies = [
        pltpu.make_async_copy(normal_ref, normal_hbm, sems.at[0]),
        pltpu.make_async_copy(tops_ref, tops_hbm, sems.at[1]),
    ]
    for copy in copies:
        copy.start()
    for copy in copies:
        copy.wait()


def finals(order, gathered):
    levels, _, heads, width = gathered.shape
    shape = (heads, (width - LANES) // (2 * levels))
    normal, tops, _ = call(
        order,
        finals_kernel,
        [gathered],
        [
            pltpu.HBM(shape, jnp.float32),
            pltpu.HBM((1, heads), jnp.float32),
            pltpu.VMEM((8, LANES), jnp.float32),
        ],
        "finals",
        scratch=[
            pltpu.VMEM(shape, jnp.float32),
            pltpu.VMEM((1, heads), jnp.float32),
            pltpu.SemaphoreType.DMA((2,)),
        ],
    )
    return normal, tops


def attention_kernel(
    queries_ref, keys_ref, values_ref, rows_ref, columns_ref, parts_ref, *refs, heads, index
):
    out_ref, sums_ref, products_ref = refs[-3:]
    tokens = queries_ref.shape[0]
    dqk, dv = queries_ref.shape[1] // heads, values_ref.shape[1] // heads
    key_columns, value_columns = pl.ds(index * dqk, dqk), pl.ds(index * dv, dv)
    tile = min(256, tokens)
    level = rows_ref[index : index + 1, :]
    causal = row_iota((tile, tile)) >= lane_iota((tile, tile))
    part_lanes = lane_iota(parts_ref.shape)
    mine = (lax.rem(part_lanes, heads) == index) & (part_lanes < 3 * heads)
    parts = jnp.where(mine, parts_ref[...], 0.0).astype(jnp.bfloat16)

    for begin in range(0, tokens, tile):
        end = begin + tile
        here = pl.ds(begin, tile)
        query = queries_ref[here, key_columns]
        running = columns_ref[here, heads + index : heads + index + 1]
        total, pieces = jnp.zeros((tile, 1), jnp.float32), []
        for low in range(0, end, tile):
            scores = lax.dot_general(
                query, keys_ref[pl.ds(low, tile), key_columns], (((1,), (1,)), ((), ())),
                preferred_element_type=jnp.float32,
            )
            attn = jnp.exp(level[:, low : low + tile] - running) * scores
            if low == begin:
                attn = jnp.where(causal, attn, 0.0)
            total = total + jnp.sum(attn, axis=1, keepdims=True)
            pieces.append(attn.astype(jnp.bfloat16))
        result = jnp.dot(
            jnp.concatenate(pieces, axis=1), values_ref[:end, value_columns], preferred_element_type=jnp.float32
        )
        product = jnp.dot(query, parts, preferred_element_type=jnp.float32)
        lanes = lane_iota((tile, LANES))
        if len(refs) > 3:
            sums_ref[here, :] = jnp.where(lanes == index, total, refs[0][here, :])
            products_ref[here, :] = refs[1][here, :] + product
        else:
            sums_ref[here, :] = jnp.where(lanes == index, total, 0.0)
            products_ref[here, :] = product
        out_ref[here, :] = result.astype(jnp.bfloat16)


def attention(order, index, queries, keys, values, rows, columns, parts, state):
    tokens = queries.shape[0]
    heads = rows.shape[0]
    dqk, dv = queries.shape[1] // heads, values.shape[1] // heads
    return call(
        order,
        functools.partial(attention_kernel, heads=heads, index=index),
        [queries, keys, values, rows, columns, parts, *state],
        [
            pltpu.VMEM((tokens, dv), jnp.bfloat16),
            pltpu.VMEM((tokens, LANES), jnp.float32),
            pltpu.VMEM((tokens, LANES), jnp.float32),
        ],
        "attention",
        mib=12,
    )


def factors_kernel(columns_ref, top_ref, sums_ref, products_ref, out_ref, *, heads, dqk):
    tokens = columns_ref.shape[0]
    tile = min(256, tokens)
    shift = lambda block, by: pltpu.roll(block, (LANES - by) % LANES, 1)
    for begin in range(0, tokens, tile):
        here = pl.ds(begin, tile)
        product = products_ref[here, :]
        product = product + shift(product, heads) + shift(product, 2 * heads)
        column = columns_ref[here, :]
        running, cumulated = shift(column, heads), shift(column, 2 * heads)
        top = top_ref[0:1, :]
        highest = jnp.maximum(running, top)
        scaling = float(dqk) ** -0.5
        local, carried = jnp.exp(running - highest), jnp.exp(top - highest)
        denominator = (local * sums_ref[here, :] + carried * product) * scaling
        divisor = jnp.maximum(jnp.abs(denominator), jnp.exp(-(cumulated + highest)))
        inverse = scaling / divisor
        out_ref[here, :] = jnp.where(
            lane_iota((tile, LANES)) < heads, local * inverse, pltpu.roll(carried * inverse, heads, 1)
        )


def factors(order, columns, top_row, sums, products, heads, dqk):
    return call(
        order,
        functools.partial(factors_kernel, heads=heads, dqk=dqk),
        [columns, top_row, sums, products],
        [pltpu.VMEM(columns.shape, jnp.float32)],
        "factors",
    )[0]


def finish_heads(queries_ref, factors_ref, refs, items, heads, out_hbm, memory, scratch, sems):
    side, _ = position()
    tokens = queries_ref.shape[0]
    dqk = queries_ref.shape[1] // heads
    dv = scratch.shape[2]
    rows = dqk // 2
    stripe = dqk // lax.axis_size(AXIS)
    tile = min(256, tokens)
    copies = []
    for at, (head, held, own, other) in enumerate(items):
        own = refs[own[0]][own[1] : own[1] + rows, :].astype(jnp.bfloat16)
        other = refs[other[0]][other[1] : other[1] + rows, :].astype(jnp.bfloat16)
        low, high = jnp.where(side == 0, own, other), jnp.where(side == 0, other, own)
        for i in range(rows // stripe):
            memory[2 * i * stripe : (2 * i + 1) * stripe, :] = low[i * stripe : (i + 1) * stripe]
            memory[(2 * i + 1) * stripe : (2 * i + 2) * stripe, :] = high[i * stripe : (i + 1) * stripe]
        prefix = memory[...]
        for begin in range(0, tokens, tile):
            here = pl.ds(begin, tile)
            local = factors_ref[here, head : head + 1]
            carried = factors_ref[here, heads + head : heads + head + 1]
            term = jnp.dot(
                queries_ref[here, head * dqk : (head + 1) * dqk], prefix, preferred_element_type=jnp.float32
            )
            value = refs[held][here, :].astype(jnp.float32)
            scratch[at, here, :] = (value * local + term * carried).astype(scratch.dtype)
            copy = pltpu.make_async_copy(
                scratch.at[at, here, :], out_hbm.at[here, pl.ds(head * dv, dv)], sems.at[len(copies)]
            )
            copy.start()
            copies.append(copy)
    return copies


def finish_kernel(queries_ref, factors_ref, *refs, items, heads):
    *_, out_hbm, token_ref, memory, scratch, sems = refs
    token_ref[...] = jnp.zeros_like(token_ref)
    for copy in finish_heads(queries_ref, factors_ref, refs, items, heads, out_hbm, memory, scratch, sems):
        copy.wait()


def finish_operands(wanted):
    operands = Operands()
    items = [
        (head, operands.place(held), operands.view(own), operands.view(other)) for head, held, own, other in wanted
    ]
    return operands, items


def finish_scratch(wanted, tokens):
    dv = wanted[0][1].shape[1]
    rows = wanted[0][2][0].shape[0] // wanted[0][2][2]
    return [
        pltpu.VMEM((2 * rows, dv), jnp.bfloat16),
        pltpu.VMEM((len(wanted), tokens, dv), jnp.bfloat16),
        pltpu.SemaphoreType.DMA((len(wanted) * max(1, tokens // 256),)),
    ]


def finish(order, wanted, queries, factor, hidden, heads):
    operands, items = finish_operands(wanted)
    tokens = queries.shape[0]
    dv = wanted[0][1].shape[1]
    arrays = [queries, factor, *operands.arrays]
    aliases = {}
    if hidden is not None:
        aliases = {len(arrays): 0}
        arrays.append((hidden, pl.ANY))
    return call(
        order,
        functools.partial(finish_kernel, items=items, heads=heads),
        arrays,
        [pltpu.HBM((tokens, heads * dv), jnp.bfloat16), pltpu.VMEM((8, LANES), jnp.float32)],
        "finish",
        mib=12,
        scratch=finish_scratch(wanted, tokens),
        aliases=aliases,
    )[0]


def entry_of(table_ref):
    return lambda row, lane: table_ref[row : row + 1, lane : lane + 1]


def row_tiles(rows):
    tile = min(16, rows)
    return [(begin, tile) for begin in range(0, rows, tile)]


def chain_kernel(table_ref, *refs, slots):
    out_ref = refs[-1]
    entry = entry_of(table_ref)
    rows = out_ref.shape[0] // len(slots)
    for i, terms in enumerate(slots):
        terms = [(place, row, entry(which, lane)) for (place, row), which, lane in terms]
        for begin, size in row_tiles(rows):
            total = None
            for place, row, weight in terms:
                term = refs[place][row + begin : row + begin + size, :] * weight
                total = term if total is None else total + term
            out_ref[i * rows + begin : i * rows + begin + size, :] = total


def first_kernel(pair_ref, keep_ref, take_ref, out_ref, *, count):
    side, _ = position()
    width = pair_ref.shape[2]
    rows = out_ref.shape[0] // count
    for i in range(count):
        top, decay = [], []
        for which in range(2):
            top.append(pair_ref[which, i : i + 1, width - LANES : width - LANES + 1])
            decay.append(pair_ref[which, i : i + 1, width - LANES + 1 : width - LANES + 2])
        own = top[0] + jnp.where(side == 0, decay[1], 0.0)
        partner = top[1] + jnp.where(side == 0, 0.0, decay[0])
        highest = jnp.maximum(own, partner)
        own, partner = jnp.exp(own - highest), jnp.exp(partner - highest)
        for begin, size in row_tiles(rows):
            here = pl.ds(i * rows + begin, size)
            out_ref[here, :] = keep_ref[here, :] * own + take_ref[here, :] * partner


def first_step(order, pair, keep, take, count):
    return call(
        order,
        functools.partial(first_kernel, count=count),
        [pair, keep, take],
        [pltpu.VMEM(keep.shape, jnp.float32)],
        "chain",
    )[0]


def chain_step(order, table, step, chunks, kept, received, earlier, levels):
    operands = Operands()
    slots = []
    for slot in range(2):
        terms = []
        lane = 2 * step + slot
        for z in range(levels - 1):
            if 0 <= step - z < len(chunks) and slot < len(chunks[step - z]):
                head = chunks[step - z][slot]
                terms.append((operands.view(kept[head]), ROW_CHAIN + 2 * z, lane))
                terms.append((operands.view(received[head]), ROW_CHAIN + 2 * z + 1, lane))
        if terms:
            if slot < earlier[2]:
                terms.append((operands.view((earlier[0], slot * earlier[1], earlier[2])), ROW_A, lane))
            slots.append(terms)
    rows, dv = earlier[1], earlier[0].shape[1]
    value = call(
        order,
        functools.partial(chain_kernel, slots=slots),
        [table, *operands.arrays],
        [pltpu.VMEM((rows * len(slots), dv), jnp.float32)],
        "chain",
    )[0]
    return value, rows, len(slots)


def prefix_kernel(table_ref, *refs, levels, pieces):
    send_ref, own_ref = refs[-2:]
    rows = send_ref.shape[0] // len(pieces)
    entry = entry_of(table_ref)
    here_row = ROW_CHAIN + 2 * levels
    picks = [entry(here_row + z, 0) for z in range(1, levels)]
    for i, (head, arrivals, (keep, keep_row), (take, take_row)) in enumerate(pieces):
        send_p, send_s = entry(ROW_SEND_P, head), entry(ROW_SEND_S, head)
        own_p, own_s = entry(ROW_OWN_P, head), entry(ROW_OWN_S, head)
        for begin, size in row_tiles(rows):
            prefix = None
            for (place, row), weight in zip(arrivals, picks):
                term = refs[place][row + begin : row + begin + size, :] * weight
                prefix = term if prefix is None else prefix + term
            here = pl.ds(i * rows + begin, size)
            send_ref[here, :] = prefix * send_p + refs[keep][keep_row + begin : keep_row + begin + size, :] * send_s
            own_ref[here, :] = prefix * own_p + refs[take][take_row + begin : take_row + begin + size, :] * own_s


def prefixes(order, table, index, chunks, arrived, kept, received, levels):
    operands = Operands()
    pieces = []
    for slot, head in enumerate(chunks[index]):
        arrivals = []
        for z in range(1, levels):
            array, rows, count = arrived[index + z - 1]
            arrivals.append(operands.view((array, slot * rows, count)))
        pieces.append((head, arrivals, operands.view(kept[head]), operands.view(received[head])))
    out = pltpu.VMEM((len(pieces) * arrived[0][1], kept[0][0].shape[1]), jnp.float32)
    return call(
        order,
        functools.partial(prefix_kernel, levels=levels, pieces=pieces),
        [table, *operands.arrays],
        [out, out],
        "prefix",
    )


def level_rows(table_ref, refs, views, level, stripe):
    entry = entry_of(table_ref)
    for head, ((keep, keep_row), (take, take_row)) in enumerate(views):
        here = lambda row: pl.ds(pl.multiple_of(row + level * stripe, stripe), stripe)
        yield (
            head,
            refs[keep][here(keep_row), :] * entry(ROW_FIN_K, head)
            + refs[take][here(take_row), :] * entry(ROW_FIN_R, head),
        )


def down_kernel(table_ref, *refs, step, levels, views, earlier):
    out_ref = refs[-1]
    stripe = out_ref.shape[1]
    _, level = position()
    target = jnp.maximum(step - levels + level, 0)
    for head, value in level_rows(table_ref, refs, views, target, stripe):
        out_ref[head] = value if earlier is None else value + refs[earlier][head]


def down(order, table, step, levels, kept, received, earlier, stripe):
    operands = Operands()
    views = [(operands.view(keep), operands.view(take)) for keep, take in zip(kept, received)]
    place = None if earlier is None else operands.place(earlier)
    return call(
        order,
        functools.partial(down_kernel, step=step, levels=levels, views=views, earlier=place),
        [table, *operands.arrays],
        [pltpu.VMEM((len(kept), stripe, kept[0][0].shape[1]), jnp.float32)],
        "down",
    )[0]


def final_kernel(table_ref, above_ref, *refs, views, prefix_views):
    *_, final_hbm, token_ref, final_ref, sem = refs
    token_ref[...] = jnp.zeros_like(token_ref)
    side, level = position()
    stripe = above_ref.shape[1]
    entry = entry_of(table_ref)
    for head, value in level_rows(table_ref, refs, views, level, stripe):
        (own, own_row), (sent, sent_row) = prefix_views[head]
        here = lambda row: pl.ds(pl.multiple_of(row + level * stripe, stripe), stripe)
        prefix = jnp.where(side == 0, refs[own][here(own_row), :], refs[sent][here(sent_row), :])
        final_ref[head] = value + prefix * entry(ROW_FIN_P, head) + above_ref[head]
    copy = pltpu.make_async_copy(final_ref, final_hbm, sem)
    copy.start()
    copy.wait()


def final_rows(order, table, above, kept, received, owns, sends):
    operands = Operands()
    views = [(operands.view(keep), operands.view(take)) for keep, take in zip(kept, received)]
    prefix_views = [(operands.view(own), operands.view(sent)) for own, sent in zip(owns, sends)]
    return call(
        order,
        functools.partial(final_kernel, views=views, prefix_views=prefix_views),
        [table, above, *operands.arrays],
        [pltpu.HBM(above.shape, jnp.float32), pltpu.VMEM((8, LANES), jnp.float32)],
        "final_rows",
        scratch=[pltpu.VMEM(above.shape, jnp.float32), pltpu.SemaphoreType.DMA],
    )[0]


def shards(queries, keys, values, input_gate, forget_gate, *, blocks):
    heads = input_gate.shape[0]
    dqk, dv = queries.shape[1] // heads, values.shape[1] // heads
    rows_of_unit = dqk // 2
    levels = blocks // 2
    across = [(i, i ^ 1) for i in range(blocks)]
    hops = lambda levels_sending, by: [(2 * z + i, 2 * (z + by) + i) for z in levels_sending for i in range(2)]
    up = lambda step: hops([z for z in range(levels - 1) if 0 <= step - z < len(chunks)], 1)
    downward = lambda step: hops([z for z in range(1, levels) if step - levels + z >= 0], -1)
    back = [(i, i ^ 1) for i in range(blocks) if i != 1]
    send = lambda value, pairs: lax.ppermute(value, AXIS, pairs)
    order = Order()
    chunks = chunks_of(heads)
    steps = len(chunks) + levels - 2

    def views_of(arrays):
        return [
            (array, slot * rows_of_unit, len(chunk))
            for array, chunk in zip(arrays, chunks)
            for slot in range(len(chunk))
        ]

    keys, first_value, rows, columns, summary = start(order, input_gate, forget_gate, keys, values)
    taken, kept = [], []

    def remember(held_values, chunk, **more):
        away, keep = memories(order, keys, columns, held_values, chunk, heads, **more)
        taken.append(send(away, across))
        kept.append(keep)

    remember(first_value, chunks[0], summary=summary)
    values, queries = load(order, [values, queries])
    remember(values, chunks[1])

    pair = pair_of(order, summary, taken[0])
    alone = len(chunks[0])
    arrived = [(send(first_step(order, pair, kept[0], taken[0], alone), up(0)), rows_of_unit, alone)]
    gathered = pair[None]
    while gathered.shape[0] < levels:
        reach = gathered.shape[0]
        more = send(gathered, [(i, (i - 2 * reach) % blocks) for i in range(blocks)])
        if len(taken) < len(chunks) - 1:
            remember(values, chunks[len(taken)])
        gathered = pack(order, [gathered, more], min(2 * reach, levels))
    while len(taken) < len(chunks) - 1:
        remember(values, chunks[len(taken)])
    table, parts, top_row = weights(order, gathered)

    attended, state = [], ()
    sends, owns, others = [], [], []
    hidden = factor = above = final_normal = tops = None
    falls = finished = 0

    def attend(count):
        nonlocal state
        for _ in range(count):
            if len(attended) < heads:
                result, *state = attention(
                    order, len(attended), queries, keys, values, rows, columns, parts, state
                )
                attended.append(result)

    def exchange():
        to_send, own = prefixes(
            order, table, len(owns), chunks, arrived, views_of(kept), views_of(taken), levels
        )
        sends.append(to_send)
        owns.append(own)
        others.append(send(to_send, back))

    def fall():
        nonlocal falls, above
        falls += 1
        above = send(
            down(order, table, falls, levels, views_of(kept), views_of(taken), above, dqk // blocks), downward(falls)
        )

    def wanted(chunk):
        return [(head, attended[head], views_of(owns)[head], views_of(others)[head]) for head in chunks[chunk]]

    def put():
        nonlocal hidden, finished
        hidden = finish(order, wanted(finished), queries, factor, hidden, heads)
        finished += 1

    plan = {1: "ma", 2: "aaaa", 3: "paadx", 4: "paFodx", 5: "pofd", 6: "XpoY"}
    for step in range(1, steps):
        value, unit_rows, count = chain_step(
            order, table, step, chunks, views_of(kept), views_of(taken), arrived[-1], levels
        )
        arrived.append((send(value, up(step)), unit_rows, count))
        for what in plan.get(step, ""):
            if what == "m":
                remember(values, chunks[-1])
            elif what == "a":
                attend(1)
            elif what == "f":
                final_normal, tops = finals(order, gathered)
            elif what == "F" and len(attended) == heads:
                factor = factors(order, columns, top_row, *state, heads, dqk)
            elif what == "p" and len(owns) + levels - 2 < step:
                exchange()
            elif what == "d" and falls < levels - 1:
                fall()
            elif what == "o" and factor is not None and finished < len(owns):
                put()
            elif what == "x" and others:
                wait(order, others[-1])
            elif what == "W":
                wait(order, taken[-1], 3e9)
            elif what == "X" and others:
                wait(order, others[-1], 3e9)
            elif what == "Y" and above is not None:
                wait(order, above, 3e9)
    attend(heads)
    if factor is None:
        factor = factors(order, columns, top_row, *state, heads, dqk)
    while len(owns) < len(chunks):
        exchange()
    while falls < levels - 1:
        fall()
    if final_normal is None:
        final_normal, tops = finals(order, gathered)
    final_memory = final_rows(
        order, table, above, views_of(kept), views_of(taken), views_of(owns), views_of(sends)
    )
    while finished < len(chunks):
        put()
    return hidden, final_memory, final_normal, tops.reshape(heads)


def solution(mesh):
    token_spec = P(("seq", "ctx"), None)
    gate_spec = P(None, ("seq", "ctx"))
    return jax.shard_map(
        functools.partial(shards, blocks=mesh.shape["ctx"]),
        mesh=mesh,
        in_specs=(token_spec, token_spec, token_spec, gate_spec, gate_spec),
        out_specs=(token_spec, P("seq", "ctx", None), P("seq", "ctx"), P("seq")),
        check_vma=False,
    )
```
